1024 devices in a mesh: row: 32 (over z_lo, y), col: 32 (over x, z_hi, core).
Axes of the slice: x: 4, y: 8, z: 16 (z_hi: 4, z_lo: 4; z = z_hi * 4 + z_lo), core: 2. Of those that a mesh axis runs over, the one named last changes fastest.
Arguments:
- a_panels: float32 [32, 32, 3, 256, 256], P('row', 'col'), may hold values from -0.375 to 0.375
- a_index: int32 [32, 32, 3], P('row', 'col'), may hold values from 0 to 16, as said below
- b_panels: float32 [32, 32, 3, 256, 256], P('row', 'col'), may hold values from -6 to 6
- b_index: int32 [32, 32, 3], P('row', 'col'), may hold values from 0 to 16, as said below
- c_index: int32 [32, 32, 6], P('row', 'col'), may hold values from 0 to 15, as said below
Outputs:
- product_blocks: float32 [32, 32, 6, 256, 256], P('row', 'col')
The draws below stay inside these ranges and needn't reach their ends.
Inputs may be any that keep to these rules, and one draw needn't show every extreme that they name: `a_index`: within one panel the occupied slots come first and hold distinct positions; every panel has at least one occupied slot; some panel is full and some is padded. `b_index`: within one panel the occupied slots come first and hold distinct positions; every panel has at least one occupied slot; some panel is full and some is padded. `c_index`: the 6 positions of one device are distinct.
All inputs are finite; a program needn't handle non-finite values.
Results may differ from the reference program's by a relative error of at most 0.0003.
Values sent between devices are 32-bit elements; how exact they have to be, the bound alone decides.
A program may use at most 128 MiB of HBM per device.

```python
import jax
import jax.numpy as jnp
from jax import lax

BS = 256
RB = 4
CB = 4
KB = 4
P_SIZE = 3
F = 6
N_ROW = 32
N_COL = 32


def pick_positions(key, device_list, chosen_positions, block_count_total, forced):
    block_scores = jax.random.randint(key, (device_list, chosen_positions), 0, 1 << 20) * chosen_positions + jnp.arange(chosen_positions)[None, :]
    extra_credit = jnp.zeros((device_list, chosen_positions), jnp.int32)
    for target_place, free_spot in enumerate(forced):
        extra_credit = extra_credit.at[0, free_spot].set((1 << 28) - target_place * (1 << 25))
    block_values, sorted_order = lax.top_k(block_scores + extra_credit, block_count_total)
    return sorted_order.astype(jnp.int32)


def panel_slots(key, chosen_positions):
    device_list = N_ROW * N_COL
    key_order, key_count = jax.random.split(key)
    sorted_order = pick_positions(key_order, device_list, chosen_positions, P_SIZE, [0])
    counts = jax.random.randint(key_count, (device_list,), 1, P_SIZE + 1)
    counts = counts.at[0].set(P_SIZE - 1).at[1].set(P_SIZE)
    slot_ids = jnp.arange(P_SIZE)[None, :]
    slots = jnp.where(slot_ids < counts[:, None], sorted_order, chosen_positions)
    return slots.astype(jnp.int32).reshape((N_ROW, N_COL, P_SIZE))


def draw_a_index(key, part):
    key = jax.random.fold_in(key, 11)
    return panel_slots(key, RB * KB)


def draw_b_index(key, part):
    key = jax.random.fold_in(key, 23)
    return panel_slots(key, KB * CB)


def draw_c_index(key, part):
    key = jax.random.fold_in(key, 37)
    sorted_order = pick_positions(key, N_ROW * N_COL, RB * CB, F, [0, RB * CB - 1])
    return sorted_order.reshape((N_ROW, N_COL, F))


def level_of(key, dims, pieces, least, largest):
    loudness = 1.0
    for position, blocks in pieces:
        steps = jax.random.uniform(jax.random.fold_in(jax.random.fold_in(key, 6), position), (blocks,), jnp.float32, least / len(pieces), largest / len(pieces))
        loudness = loudness * jnp.repeat(jnp.exp(steps), dims[position] // blocks).reshape((-1,) + (1,) * (len(dims) - 1 - position))
    return loudness


def bell_draw(own_key, dims, deviation, limit, cuts=(), kind=jnp.bfloat16):
    loudness = level_of(own_key, dims, cuts, -0.22, 0.18) if cuts else 1.0
    drawn = jax.random.normal(own_key, dims, jnp.float32) * deviation * loudness
    return jnp.minimum(jnp.maximum(drawn, -limit), limit).astype(kind)


def setup_inputs(seed: int = 0) -> dict:
    keys = jax.random.split(jax.random.key(seed), 6)
    a_panels = bell_draw(keys[0], (N_ROW, N_COL, P_SIZE, BS, BS), BS ** -0.5, 0.375, ((0, 32), (1, 32)), jnp.float32)
    a_index = draw_a_index(jax.random.fold_in(keys[5], 71), 0)
    b_panels = bell_draw(keys[2], (N_ROW, N_COL, P_SIZE, BS, BS), 1.0, 6.0, ((0, 32), (1, 32)), jnp.float32)
    b_index = draw_b_index(jax.random.fold_in(keys[5], 71), 0)
    c_index = draw_c_index(jax.random.fold_in(keys[5], 71), 0)
    return dict(a_panels=a_panels, a_index=a_index, b_panels=b_panels, b_index=b_index, c_index=c_index)


def pair_product(a_blocks, a_slots, b_blocks, b_slots, c_slots):
    a_valid = a_slots < RB * KB
    a_inner = a_slots % KB
    a_row = a_slots // KB
    b_valid = b_slots < KB * CB
    b_inner = b_slots // CB
    b_col = b_slots % CB
    prods = jnp.einsum("pxy,qyz->pqxz", a_blocks.astype(jnp.float32), b_blocks.astype(jnp.float32), precision=lax.Precision.HIGHEST)
    matched = (a_inner[:, None] == b_inner[None, :]) & a_valid[:, None] & b_valid[None, :]
    target = a_row[:, None] * CB + b_col[None, :]
    select = ((target[None, :, :] == c_slots[:, None, None]) & matched[None, :, :]).astype(jnp.float32)
    return jnp.einsum("fpq,pqxz->fxz", select, prods, precision=lax.Precision.HIGHEST)


def reference(a_panels, a_index, b_panels, b_index, c_index):
    a_later = jnp.roll(a_panels, -1, axis=1)
    a_later_index = jnp.roll(a_index, -1, axis=1)
    b_later = jnp.roll(b_panels, -1, axis=0)
    b_later_index = jnp.roll(b_index, -1, axis=0)

    def flatten(array):
        return array.reshape((N_ROW * N_COL,) + array.shape[2:])

    def device_blocks(items):
        first_a, first_ai, first_b, first_bi, later_a, later_ai, later_b, later_bi, kept = items
        return pair_product(first_a, first_ai, first_b, first_bi, kept) + pair_product(later_a, later_ai, later_b, later_bi, kept)

    stacked = (flatten(a_panels), flatten(a_index), flatten(b_panels), flatten(b_index), flatten(a_later), flatten(a_later_index), flatten(b_later), flatten(b_later_index), flatten(c_index))
    result = lax.map(device_blocks, stacked)
    return result.reshape((N_ROW, N_COL, F, BS, BS))
```

```python
import jax
import jax.numpy as jnp
from jax import lax
from jax.experimental import pallas as pl
from jax.experimental.pallas import tpu as pltpu
from jax.sharding import PartitionSpec as P

BS = 256
SLOTS = 3
F = 6
ROWS = SLOTS * BS
LINES = 8
ZS = 16
DIRECT = 576
PIECE = ROWS // LINES
RELAYED = ROWS - DIRECT
SPREAD = True

MESH = pl.DeviceIdType.MESH
ANY = pl.BlockSpec(memory_space=pl.ANY)
SMEM = pl.BlockSpec(memory_space=pltpu.SMEM)


def exchange_kernel(a_ref, b_ref, ai_ref, bi_ref, a2_ref, b2_ref, ai2_ref, bi2_ref,
                    msg, relay, first, second, a_sems, i_sems, r_sems, b_sems, l_sems, f_sems, g_sems):
    row, col = lax.axis_index("row"), lax.axis_index("col")
    y, z_lo = lax.rem(row, LINES), lax.div(row, LINES)
    core, chip = lax.rem(col, 2), lax.div(col, 2)
    z_hi, x = lax.rem(chip, 4), lax.div(chip, 4)
    z = z_hi * 4 + z_lo

    def place(px, py, pz, pcore):
        pz = lax.rem(pz, ZS)
        return (lax.rem(pz, 4) * LINES + py, (lax.rem(px, 4) * 4 + lax.div(pz, 4)) * 2 + pcore)

    a_to, a_from = (row, lax.rem(col + 31, 32)), (row, lax.rem(col + 1, 32))
    b_to, b_from = (lax.rem(row + 31, 32), col), (lax.rem(row + 1, 32), col)
    relay_to, relay_from = place(x, y, z + 6, 0), place(x, y, z + 10, 0)
    origin_z = lax.rem(z + 10, ZS)
    relay_end = place(x + jnp.where(origin_z < 4, 3, 0), y, origin_z + 12, 1)
    relay_last = place(x + jnp.where(z_hi == 3, 1, 0), y, z + 10, 0)
    z_down, z_up = lax.rem(z_lo + 3, 4) * LINES, lax.rem(z_lo + 1, 4) * LINES
    here = z_lo * LINES

    barrier = pltpu.get_barrier_semaphore()

    def greet(device):
        pl.semaphore_signal(barrier, inc=1, device_id=device, device_id_type=MESH)

    greet(a_from)
    greet(b_from)

    @pl.when(core == 0)
    def _():
        greet(relay_from)

    @pl.when(core == 1)
    def _():
        greet(relay_last)

    @pl.when(y != 0)
    def _():
        greet((here, col))

    greet((z_up + y, col))

    @pl.when(y == LINES - 1)
    def _():
        for line in range(LINES - 1):
            greet((here + line, col))

    ints = (8, 128)
    lane = lax.broadcasted_iota(jnp.int32, ints, 1)
    for which, source in enumerate((ai_ref, bi_ref)):
        packed = jnp.zeros(ints, jnp.int32)
        for slot in range(SLOTS):
            packed = jnp.where(lane == slot, source[0, 0, slot], packed)
        msg[which] = packed

    dests = 3 + jnp.where(core == 0, 2, 0)
    dests = dests + jnp.where(y != LINES - 1, 1, 0) + jnp.where(y == 0, LINES - 1, 0)
    pl.semaphore_wait(barrier, dests)

    def remote(src, dst, sems, device):
        return pltpu.make_async_remote_copy(src_ref=src, dst_ref=dst, send_sem=sems.at[0], recv_sem=sems.at[1],
                                            device_id=device, device_id_type=MESH)

    head, tail = pl.ds(0, DIRECT), pl.ds(DIRECT, RELAYED)
    a_rest = remote(a_ref.at[tail], a2_ref.at[tail], a_sems.at[1], a_to)
    a_out = remote(a_ref.at[tail], relay, r_sems.at[0], relay_to)
    a_on = remote(relay, a2_ref.at[tail], a_sems.at[1], relay_end)
    a_main = remote(a_ref.at[head], a2_ref.at[head], a_sems.at[0], a_to)
    ints_a = remote(msg.at[0], ai2_ref, i_sems.at[0], a_to)
    ints_b = remote(msg.at[1], bi2_ref, i_sems.at[1], b_to)
    b_main = remote(b_ref, b2_ref, b_sems, b_to)

    @pl.when(core == 0)
    def _():
        a_out.start()

    @pl.when(core == 1)
    def _():
        a_rest.start()

    @pl.when(y != 0)
    def _():
        b_main.start()

    def part(line):
        return pl.ds(line * PIECE, PIECE)

    def first_leg(line):
        return pltpu.make_async_remote_copy(
            src_ref=b_ref.at[part(line)], dst_ref=first, send_sem=f_sems.at[line], recv_sem=l_sems.at[0],
            device_id=(here + line, col), device_id_type=MESH)

    lead_leg = remote(b_ref.at[part(0)], second, l_sems.at[pl.ds(1, 2)], (z_down, col))
    mid_leg = remote(first, second, l_sems.at[pl.ds(1, 2)], (z_down + y, col))
    end_leg = remote(first, b2_ref.at[part(LINES - 1)], l_sems.at[pl.ds(1, 2)], (z_down + y, col))
    my_part = pl.ds(pl.multiple_of(y * PIECE, PIECE), PIECE)
    last_leg = pltpu.make_async_remote_copy(
        src_ref=second, dst_ref=b2_ref.at[my_part], send_sem=l_sems.at[3], recv_sem=g_sems.at[y],
        device_id=(here + LINES - 1, col), device_id_type=MESH)

    @pl.when(y == 0)
    def _():
        lead_leg.start()
        for line in range(1, LINES):
            first_leg(line).start()

    a_main.start()
    ints_a.start()
    ints_b.start()

    @pl.when(y != 0)
    def _():
        first_leg(1).wait_recv()

    @pl.when((y != 0) & (y != LINES - 1))
    def _():
        mid_leg.start()

    @pl.when(y == LINES - 1)
    def _():
        end_leg.start()

    @pl.when(y != LINES - 1)
    def _():
        mid_leg.wait_recv()
        last_leg.start()

    @pl.when(core == 0)
    def _():
        a_out.wait_recv()
        a_on.start()

    mid_leg.wait_send()

    @pl.when(y == LINES - 1)
    def _():
        end_leg.wait_recv()
        for line in range(LINES - 1):
            pltpu.make_async_remote_copy(
                src_ref=second, dst_ref=b2_ref.at[part(line)], send_sem=l_sems.at[3], recv_sem=g_sems.at[line],
                device_id=(here + LINES - 1, col), device_id_type=MESH).wait_recv()

    @pl.when(y != LINES - 1)
    def _():
        last_leg.wait_send()
        b_main.wait_recv()

    @pl.when(y != 0)
    def _():
        b_main.wait_send()

    @pl.when(y == 0)
    def _():
        for line in range(1, LINES):
            first_leg(line).wait_send()

    ints_a.wait()
    ints_b.wait()
    a_main.wait()

    @pl.when(core == 0)
    def _():
        a_out.wait_send()

    a_rest.wait()


def exchange(a, b, a_index, b_index):
    panel = jax.ShapeDtypeStruct((ROWS, BS), jnp.float32)
    ints = jax.ShapeDtypeStruct((8, 128), jnp.int32)
    dma = pltpu.SemaphoreType.DMA
    return pl.pallas_call(
        exchange_kernel,
        out_shape=(panel, panel, ints, ints),
        in_specs=[ANY, ANY, SMEM, SMEM],
        out_specs=(ANY, ANY, ANY, ANY),
        scratch_shapes=[
            pltpu.VMEM((2, 8, 128), jnp.int32),
            pltpu.VMEM((RELAYED, BS), jnp.float32),
            pltpu.VMEM((PIECE, BS), jnp.float32),
            pltpu.VMEM((PIECE, BS), jnp.float32),
            dma((2, 2)),
            dma((2, 2)),
            dma((1, 2)),
            dma((2,)),
            dma((4,)),
            dma((LINES,)),
            dma((LINES,)),
        ],
        compiler_params=pltpu.CompilerParams(collective_id=0, has_side_effects=True),
        cost_estimate=pl.CostEstimate(flops=0, bytes_accessed=4 * ROWS * BS * 4, transcendentals=0),
        name="exchange",
    )(a, b, a_index, b_index)


def product_kernel(a0, b0, a1, b1, ai0, bi0, ai1, bi1, ci, out, va, vb, acc, plan, a_sem, b_sem, out_sem):
    need_a = [jnp.int32(0)] * (2 * SLOTS)
    need_b = [jnp.int32(0)] * (2 * SLOTS)
    count = jnp.int32(0)
    touched = [jnp.int32(0)] * F
    kept = [ci[0, 0, f] for f in range(F)]
    steps = (
        ([ai0[0, 0, p] for p in range(SLOTS)], [bi0[0, 0, q] for q in range(SLOTS)]),
        ([ai1[0, p] for p in range(SLOTS)], [bi1[0, q] for q in range(SLOTS)]),
    )
    for step, (a_slots, b_slots) in enumerate(steps):
        for p, v in enumerate(a_slots):
            for q, w in enumerate(b_slots):
                meet = (v < 16) & (w < 16) & ((v & 3) == (w >> 2))
                target = (v & 12) + (w & 3)
                place = jnp.int32(0)
                hit = jnp.int32(0)
                for f in range(F):
                    mine = (meet & (kept[f] == target)).astype(jnp.int32)
                    place = place + f * mine
                    hit = hit + mine
                    touched[f] = touched[f] | mine
                plan[count] = ((step * SLOTS + p) * 8 + step * SLOTS + q) * 8 + place
                count = count + hit
                need_a[step * SLOTS + p] |= hit
                need_b[step * SLOTS + q] |= hit

    def fetches():
        for step, (a, b) in enumerate(((a0, b0), (a1, b1))):
            for p in range(SLOTS):
                n = step * SLOTS + p
                part = pl.ds(p * BS, BS)
                yield need_a[n], pltpu.make_async_copy(a.at[part], va.at[n], a_sem.at[n])
                yield need_b[n], pltpu.make_async_copy(b.at[part], vb.at[n], b_sem.at[n])

    for need, copy in fetches():
        pl.when(need != 0)(copy.start)

    writes = [pltpu.make_async_copy(acc.at[f], out.at[f], out_sem.at[f]) for f in range(F)]
    for f in range(F):
        acc[f] = jnp.zeros((BS, BS), jnp.float32)
        pl.when(touched[f] == 0)(writes[f].start)

    for need, copy in fetches():
        pl.when(need != 0)(copy.wait)

    def pair(t, carry):
        entry = plan[t]
        a, b = va[entry >> 6], vb[(entry >> 3) & 7]
        f = entry & 7
        a_hi, b_hi = a.astype(jnp.bfloat16), b.astype(jnp.bfloat16)
        a_lo = (a - a_hi.astype(jnp.float32)).astype(jnp.bfloat16)
        b_lo = (b - b_hi.astype(jnp.float32)).astype(jnp.bfloat16)

        def dot(left, right):
            return jnp.dot(left, right, preferred_element_type=jnp.float32)

        acc[f] += dot(a_hi, b_hi) + (dot(a_hi, b_lo) + dot(a_lo, b_hi))
        return carry

    lax.fori_loop(0, count, pair, 0)
    for f in range(F):
        pl.when(touched[f] != 0)(writes[f].start)
    for f in range(F):
        writes[f].wait()


def products(a0, b0, a1, b1, ai0, bi0, ai1, bi1, ci):
    dma = pltpu.SemaphoreType.DMA
    return pl.pallas_call(
        product_kernel,
        out_shape=jax.ShapeDtypeStruct((F, BS, BS), jnp.float32),
        in_specs=[ANY] * 4 + [SMEM] * 5,
        out_specs=ANY,
        scratch_shapes=[
            pltpu.VMEM((2 * SLOTS, BS, BS), jnp.float32),
            pltpu.VMEM((2 * SLOTS, BS, BS), jnp.float32),
            pltpu.VMEM((F, BS, BS), jnp.float32),
            pltpu.SMEM((128,), jnp.int32),
            dma((2 * SLOTS,)),
            dma((2 * SLOTS,)),
            dma((F,)),
        ],
        compiler_params=pltpu.CompilerParams(vmem_limit_bytes=16 * 1024 * 1024),
        cost_estimate=pl.CostEstimate(flops=6 * BS ** 3, bytes_accessed=12 * BS * BS * 4, transcendentals=0),
        name="products",
    )(a0, b0, a1, b1, ai0, bi0, ai1, bi1, ci)


def per_device(a_panels, a_index, b_panels, b_index, c_index):
    a0 = a_panels.reshape(ROWS, BS)
    b0 = b_panels.reshape(ROWS, BS)
    a1, b1, ai1, bi1 = exchange(a0, b0, a_index, b_index)
    blocks = products(a0, b0, a1, b1, a_index, b_index, ai1, bi1, c_index)
    return blocks[None, None]


def solution(mesh):
    return jax.shard_map(
        per_device,
        mesh=mesh,
        in_specs=(
            P("row", "col", None, None, None),
            P("row", "col", None),
            P("row", "col", None, None, None),
            P("row", "col", None),
            P("row", "col", None),
        ),
        out_specs=P("row", "col", None, None, None),
        check_vma=False,
    )
```

```python
import jax
import jax.numpy as jnp
from jax import lax
from jax.experimental import pallas as pl
from jax.experimental.pallas import tpu as pltpu
from jax.sharding import PartitionSpec as P

BS = 256
SLOTS = 3
F = 6
ROWS = SLOTS * BS
LINES = 8
ZS = 16
CHUNK = 96
SHARE = (4, 0, 2, 0)
MOST = max(1, max(SHARE))
UP = 5
PIECE = ROWS // LINES
VMEM = 60 * 1024 * 1024

MESH = pl.DeviceIdType.MESH
ANY = pl.BlockSpec(memory_space=pl.ANY)
HBM = pl.BlockSpec(memory_space=pltpu.HBM)
SMEM = pl.BlockSpec(memory_space=pltpu.SMEM)


def exchange_kernel(a_ref, b_ref, ai_ref, bi_ref, a2_ref, b2_ref, i2_ref, msg, relay, first, second,
                    a_sems, i_sems, up_send, up_recv, on_send, on_recv, b_sems, f_sems, s_sems, h_sems, m_sems, t_sems, g_sems,
                    ready):
    row, col = lax.axis_index("row"), lax.axis_index("col")
    y, z_lo = lax.rem(row, LINES), lax.div(row, LINES)
    core, chip = lax.rem(col, 2), lax.div(col, 2)
    z_hi, x = lax.rem(chip, 4), lax.div(chip, 4)
    z = z_hi * 4 + z_lo
    core0, core1 = core == 0, core == 1

    def place(px, py, pz, pcore):
        pz = lax.rem(pz, ZS)
        return (lax.rem(pz, 4) * LINES + py, (lax.rem(px, 4) * 4 + lax.div(pz, 4)) * 2 + pcore)

    def when(*conditions):
        whole = conditions[0]
        for condition in conditions[1:]:
            whole = whole & condition
        return pl.when(whole)

    def one(*conditions):
        whole = conditions[0]
        for condition in conditions[1:]:
            whole = whole & condition
        return jnp.where(whole, 1, 0)

    a_to, a_from = (row, lax.rem(col + 31, 32)), (row, lax.rem(col + 1, 32))
    relay_to = place(x, y, z + UP, 0)
    sender_z = lax.rem(z + ZS - UP, ZS)
    sender_hi = lax.div(sender_z, 4)
    sender = place(x, y, z + ZS - UP, 0)
    relay_end = place(x + jnp.where(sender_hi == 0, 3, 0), y, sender_z + 12, 1)
    last_relay = place(x + jnp.where(z_hi == 3, 1, 0), y, z + 4 + UP, 0)
    from_hi = lax.rem(z_hi + 1, 4)

    def relayed(group):
        found = group < 0
        for g in range(4):
            if SHARE[g]:
                found = found | (group == g)
        return found

    sends_up, relays, gets_up = core0 & relayed(z_hi), core0 & relayed(sender_hi), core1 & relayed(from_hi)
    up_late = z + UP < ZS
    in_late = z >= UP
    on_late = z < ZS - 4 - UP + 2
    got_late = z >= 12 - UP
    down_late, end_late = z_hi == 0, z_hi == 3

    z_down, z_up = lax.rem(z_lo + 3, 4) * LINES, lax.rem(z_lo + 1, 4) * LINES
    here = z_lo * LINES
    top, bottom = y == 0, y == LINES - 1
    b_to = (lax.rem(row + 31, 32), col)
    b_from = (lax.rem(row + 1, 32), col)
    col0, col1 = col - core, col - core + 1

    barrier = pltpu.get_barrier_semaphore()

    def greet(device):
        pl.semaphore_signal(barrier, inc=1, device_id=device, device_id_type=MESH)

    @when(~bottom)
    def _():
        greet(b_from)

    @when(core0)
    def _():
        greet(a_from)

    @when(core1, ~end_late)
    def _():
        greet(a_from)

    @when(core0, down_late)
    def _():
        greet(a_to)

    @when(sends_up, up_late)
    def _():
        greet(relay_to)

    @when(relays, ~in_late)
    def _():
        greet(sender)

    @when(relays, on_late)
    def _():
        greet(relay_end)

    @when(gets_up, ~got_late)
    def _():
        greet(last_relay)

    @when(top)
    def _():
        for line in range(1, LINES):
            greet((here + line, col1))
        greet((z_down, col1))
        greet(b_to)

    @when(core1, ~top, ~bottom)
    def _():
        greet((z_up + y, col1))

    @when(bottom)
    def _():
        for line in range(LINES - 1):
            greet((here + line, col1))
        greet((z_up + LINES - 1, col1))

    ints = (8, 128)
    lane = lax.broadcasted_iota(jnp.int32, ints, 1)
    for which, source in enumerate((ai_ref, bi_ref)):
        packed = jnp.zeros(ints, jnp.int32)
        for slot in range(SLOTS):
            packed = jnp.where(lane == slot, source[0, 0, slot], packed)
        msg[which] = packed

    greetings = one(~top) + one(core1) + one(core0, ~down_late) + one(core1, end_late)
    greetings = greetings + one(sends_up, ~up_late) + one(relays, in_late) + one(relays, ~on_late)
    greetings = greetings + one(gets_up, got_late) + 4 * one(core1) + one(core1, ~top, ~bottom)
    greetings = greetings + one(bottom)
    @when(greetings > 0)
    def _():
        pl.semaphore_wait(barrier, greetings)

    def tell(which, device):
        pl.semaphore_signal(ready.at[which], inc=1, device_id=device, device_id_type=MESH)

    @when(core1, end_late)
    def _():
        tell(0, a_from)

    @when(core1, ~top)
    def _():
        tell(3, (here, col0))
        tell(3, (here, col1))

    @when(core1, top)
    def _():
        tell(3, (z_up, col0))
        tell(3, (z_up, col1))

    @when(bottom)
    def _():
        tell(3, b_from)

    @when(relays, in_late)
    def _():
        tell(1, sender)

    @when(gets_up, got_late)
    def _():
        tell(2, last_relay)

    def remote(src, dst, send, recv, device):
        return pltpu.make_async_remote_copy(src_ref=src, dst_ref=dst, send_sem=send, recv_sem=recv,
                                            device_id=device, device_id_type=MESH)

    def head(g):
        rows = pl.ds(0, ROWS - SHARE[g] * CHUNK)
        return remote(a_ref.at[rows], a2_ref.at[rows], a_sems.at[0], a_sems.at[1], a_to)

    def chunk_rows(g, n):
        return pl.ds(ROWS - SHARE[g] * CHUNK + n * CHUNK, CHUNK)

    def slot_rows(n):
        return pl.ds(n * CHUNK, CHUNK)

    def up(g, n):
        return remote(a_ref.at[chunk_rows(g, n)], relay.at[slot_rows(n)], up_send.at[n], up_recv.at[n], relay_to)

    def on(g, n):
        return remote(relay.at[slot_rows(n)], a2_ref.at[chunk_rows(g, n)], on_send.at[n], on_recv.at[n], relay_end)

    whole = remote(a_ref, a2_ref, a_sems.at[0], a_sems.at[1], a_to)
    ints_a = remote(msg.at[0], i2_ref.at[0], i_sems.at[0], i_sems.at[1], a_to)
    ints_b = remote(msg.at[1], i2_ref.at[1], i_sems.at[2], i_sems.at[3], b_to)
    b_main = remote(b_ref, b2_ref, b_sems.at[0], b_sems.at[1], b_to)

    def part(line):
        return pl.ds(line * PIECE, PIECE)

    my_part = pl.ds(pl.multiple_of(y * PIECE, PIECE), PIECE)

    def leg_y(line, c):
        return remote(b_ref.at[part(line)], first.at[c], f_sems.at[line], h_sems.at[c], (here + line, col1))

    def leg_z(c):
        return remote(b_ref.at[part(0)], second.at[c], f_sems.at[0], s_sems.at[c], (z_down, col1))

    def then_z(c):
        return remote(first.at[c], second.at[c], m_sems.at[c], s_sems.at[c], (z_down + y, col1))

    def then_end(c):
        return remote(first.at[c], b2_ref.at[part(LINES - 1)], m_sems.at[c], g_sems.at[LINES - 1],
                      (z_down + LINES - 1, col0 + c))

    def then_y(c):
        return remote(second.at[c], b2_ref.at[my_part], t_sems.at[c], g_sems.at[y], (here + LINES - 1, col0 + c))

    def arrival(line):
        return remote(second.at[0], b2_ref.at[part(line)], t_sems.at[0], g_sems.at[line], (here, col))

    @when(core1)
    def _():
        whole.start()

    @when(~top)
    def _():
        b_main.start()
        ints_b.start()

    @when(core1)
    def _():
        ints_a.start()

    for g in range(1, 4):
        @when(core0, z_hi == g)
        def _():
            ints_a.start()
            head(g).start()

    for c in range(2):
        @when(top, core == c)
        def _():
            pl.semaphore_wait(ready.at[3], LINES + 1)
            for line in (4, 3, 5, 2, 6, 1, 7):
                leg_y(line, c).start()
            leg_z(c).start()
            ints_b.start()

    for g in range(4):
        if SHARE[g]:
            @when(core0, z_hi == g)
            def _():
                @when(up_late)
                def _():
                    pl.semaphore_wait(ready.at[1], 1)

                for n in range(SHARE[g]):
                    up(g, n).start()

    @when(core0, down_late)
    def _():
        pl.semaphore_wait(ready.at[0], 1)
        ints_a.start()
        head(0).start()

    for g in range(4):
        if SHARE[g]:
            @when(core0, sender_hi == g)
            def _():
                @when(on_late)
                def _():
                    pl.semaphore_wait(ready.at[2], 1)

                for n in range(SHARE[g]):
                    up(g, n).wait_recv()
                    on(g, n).start()

    for c in range(2):
        @when(core1, ~top)
        def _():
            leg_y(1, c).wait_recv()

        @when(core1, ~top, ~bottom)
        def _():
            then_z(c).start()

        @when(core1, bottom)
        def _():
            then_end(c).start()

    for c in range(2):
        @when(core1, ~bottom)
        def _():
            leg_z(c).wait_recv()
            then_y(c).start()

    ints_a.wait()
    ints_b.wait()

    @when(core1)
    def _():
        whole.wait_send()

    @when(core0)
    def _():
        whole.wait_recv()

    @when(~top)
    def _():
        b_main.wait_send()

    @when(~bottom)
    def _():
        b_main.wait_recv()

    @when(top)
    def _():
        leg_z(0).wait_send()
        for line in range(1, LINES):
            leg_y(line, 0).wait_send()

    for c in range(2):
        @when(core1, ~top)
        def _():
            then_z(c).wait_send()

        @when(core1, ~bottom)
        def _():
            then_y(c).wait_send()

    @when(bottom)
    def _():
        for line in range(LINES):
            arrival(line).wait_recv()

    for g in range(4):
        @when(core0, z_hi == g)
        def _():
            for n in range(SHARE[g]):
                up(g, n).wait_send()
            head(g).wait_send()

        @when(core0, sender_hi == g)
        def _():
            for n in range(SHARE[g]):
                on(g, n).wait_send()

        @when(core1, from_hi == g)
        def _():
            head(g).wait_recv()
            for n in range(SHARE[g]):
                on(g, n).wait_recv()


def exchange(a, b, a_index, b_index):
    panel = jax.ShapeDtypeStruct((ROWS, BS), jnp.float32)
    ints = jax.ShapeDtypeStruct((2, 8, 128), jnp.int32)
    dma = pltpu.SemaphoreType.DMA
    return pl.pallas_call(
        exchange_kernel,
        out_shape=(panel, panel, ints),
        in_specs=[HBM, HBM, SMEM, SMEM],
        out_specs=(HBM, HBM, HBM),
        scratch_shapes=[
            pltpu.VMEM((2, 8, 128), jnp.int32),
            pltpu.VMEM((MOST * CHUNK, BS), jnp.float32),
            pltpu.VMEM((2, PIECE, BS), jnp.float32),
            pltpu.VMEM((2, PIECE, BS), jnp.float32),
            dma((2,)),
            dma((4,)),
            dma((MOST,)),
            dma((MOST,)),
            dma((MOST,)),
            dma((MOST,)),
            dma((2,)),
            dma((LINES,)),
            dma((2,)),
            dma((2,)),
            dma((2,)),
            dma((2,)),
            dma((LINES,)),
            pltpu.SemaphoreType.REGULAR((4,)),
        ],
        compiler_params=pltpu.CompilerParams(collective_id=0, has_side_effects=True, vmem_limit_bytes=VMEM),
        cost_estimate=pl.CostEstimate(flops=0, bytes_accessed=4 * ROWS * BS * 4, transcendentals=0),
        name="exchange",
    )(a, b, a_index, b_index)


def product_kernel(a0, b0, a1, b1, ai0, bi0, i1, ci, out, va, vb, acc, later, plan, a_sem, b_sem, out_sem, i_sem):
    fetch = pltpu.make_async_copy(i1, later, i_sem)
    fetch.start()
    for f in range(F):
        acc[f] = jnp.zeros((BS, BS), jnp.float32)
    fetch.wait()
    need_a = [jnp.int32(0)] * (2 * SLOTS)
    need_b = [jnp.int32(0)] * (2 * SLOTS)
    count = jnp.int32(0)
    touched = [jnp.int32(0)] * F
    kept = [ci[0, 0, f] for f in range(F)]
    steps = (
        ([ai0[0, 0, p] for p in range(SLOTS)], [bi0[0, 0, q] for q in range(SLOTS)]),
        ([later[0, 0, p] for p in range(SLOTS)], [later[1, 0, q] for q in range(SLOTS)]),
    )
    for step, (a_slots, b_slots) in enumerate(steps):
        for p, v in enumerate(a_slots):
            for q, w in enumerate(b_slots):
                meet = (v < 16) & (w < 16) & ((v & 3) == (w >> 2))
                target = (v & 12) + (w & 3)
                place = jnp.int32(0)
                hit = jnp.int32(0)
                for f in range(F):
                    mine = (meet & (kept[f] == target)).astype(jnp.int32)
                    place = place + f * mine
                    hit = hit + mine
                    touched[f] = touched[f] | mine
                plan[count] = ((step * SLOTS + p) * 8 + step * SLOTS + q) * 8 + place
                count = count + hit
                need_a[step * SLOTS + p] |= hit
                need_b[step * SLOTS + q] |= hit

    def fetches():
        for step, (a, b) in enumerate(((a0, b0), (a1, b1))):
            for p in range(SLOTS):
                n = step * SLOTS + p
                part = pl.ds(p * BS, BS)
                yield need_a[n], pltpu.make_async_copy(a.at[part], va.at[n], a_sem.at[n])
                yield need_b[n], pltpu.make_async_copy(b.at[part], vb.at[n], b_sem.at[n])

    for need, copy in fetches():
        pl.when(need != 0)(copy.start)

    writes = [pltpu.make_async_copy(acc.at[f], out.at[f], out_sem.at[f]) for f in range(F)]
    for f in range(F):
        pl.when(touched[f] == 0)(writes[f].start)

    for need, copy in fetches():
        pl.when(need != 0)(copy.wait)

    def pair(t, carry):
        entry = plan[t]
        a, b = va[entry >> 6], vb[(entry >> 3) & 7]
        f = entry & 7
        a_hi, b_hi = a.astype(jnp.bfloat16), b.astype(jnp.bfloat16)
        a_lo = (a - a_hi.astype(jnp.float32)).astype(jnp.bfloat16)
        b_lo = (b - b_hi.astype(jnp.float32)).astype(jnp.bfloat16)

        def dot(left, right):
            return jnp.dot(left, right, preferred_element_type=jnp.float32)

        acc[f] += dot(a_hi, b_hi) + (dot(a_hi, b_lo) + dot(a_lo, b_hi))
        return carry

    lax.fori_loop(0, count, pair, 0)
    for f in range(F):
        pl.when(touched[f] != 0)(writes[f].start)
    for f in range(F):
        writes[f].wait()


def products(a0, b0, a1, b1, ai0, bi0, i1, ci):
    dma = pltpu.SemaphoreType.DMA
    return pl.pallas_call(
        product_kernel,
        out_shape=jax.ShapeDtypeStruct((F, BS, BS), jnp.float32),
        in_specs=[ANY, ANY, HBM, HBM, SMEM, SMEM, HBM, SMEM],
        out_specs=ANY,
        scratch_shapes=[
            pltpu.VMEM((2 * SLOTS, BS, BS), jnp.float32),
            pltpu.VMEM((2 * SLOTS, BS, BS), jnp.float32),
            pltpu.VMEM((F, BS, BS), jnp.float32),
            pltpu.SMEM((2, 8, 128), jnp.int32),
            pltpu.SMEM((128,), jnp.int32),
            dma((2 * SLOTS,)),
            dma((2 * SLOTS,)),
            dma((F,)),
            dma,
        ],
        compiler_params=pltpu.CompilerParams(vmem_limit_bytes=VMEM),
        cost_estimate=pl.CostEstimate(flops=6 * BS ** 3, bytes_accessed=12 * BS * BS * 4, transcendentals=0),
        name="products",
    )(a0, b0, a1, b1, ai0, bi0, i1, ci)


def per_device(a_panels, a_index, b_panels, b_index, c_index):
    a0 = a_panels.reshape(ROWS, BS)
    b0 = b_panels.reshape(ROWS, BS)
    a1, b1, i1 = exchange(a0, b0, a_index, b_index)
    blocks = products(a0, b0, a1, b1, a_index, b_index, i1, c_index)
    return blocks[None, None]


def solution(mesh):
    return jax.shard_map(
        per_device,
        mesh=mesh,
        in_specs=(
            P("row", "col", None, None, None),
            P("row", "col", None),
            P("row", "col", None, None, None),
            P("row", "col", None),
            P("row", "col", None),
        ),
        out_specs=P("row", "col", None, None, None),
        check_vma=False,
    )
```

```python
import jax
import jax.numpy as jnp
from jax import lax
from jax.experimental import pallas as pl
from jax.experimental.pallas import tpu as pltpu
from jax.sharding import PartitionSpec as P

BS = 256
SLOTS = 3
F = 6
ROWS = SLOTS * BS
LINES = 8
ZS = 16
CHUNK = 96
SHARE = (4, 4, 4, 4, 0, 0, 0, 2, 2, 2, 0, 2, 0, 0, 0, 0)
COUNTS = sorted(set(SHARE))
TURNS = False
FIRST = False
MOST = max(1, max(SHARE))
UP = 5
PIECE = ROWS // LINES
VMEM = 60 * 1024 * 1024

NEED_A = SLOTS * SLOTS
NEED_B = NEED_A + SLOTS
TOUCHED = NEED_B + SLOTS
BEGUN = TOUCHED + F
PLAN = BEGUN + F
HALF = F // 2

MESH = pl.DeviceIdType.MESH
HBM = pl.BlockSpec(memory_space=pltpu.HBM)
SMEM = pl.BlockSpec(memory_space=pltpu.SMEM)


def block_product(a, b):
    a_hi, b_hi = a.astype(jnp.bfloat16), b.astype(jnp.bfloat16)
    a_lo = (a - a_hi.astype(jnp.float32)).astype(jnp.bfloat16)
    b_lo = (b - b_hi.astype(jnp.float32)).astype(jnp.bfloat16)

    def dot(left, right):
        return jnp.dot(left, right, preferred_element_type=jnp.float32)

    return dot(a_hi, b_hi) + (dot(a_hi, b_lo) + dot(a_lo, b_hi))


def plan_later(slots, kept, plan):
    need_b = [jnp.int32(0)] * SLOTS
    touched = [jnp.int32(0)] * F
    for p in range(SLOTS):
        v = slots[0, 0, p]
        need_a = jnp.int32(0)
        for q in range(SLOTS):
            w = slots[1, 0, q]
            target = jnp.where((v < 16) & (w < 16) & ((v & 3) == (w >> 2)), (v & 12) + (w & 3), -1)
            place = jnp.int32(F)
            for f in range(F):
                mine = kept[0, 0, f] == target
                place = jnp.where(mine, f, place)
                touched[f] = jnp.where(mine, 1, touched[f])
            hit = jnp.where(place < F, 1, 0)
            plan[p * SLOTS + q] = place
            need_a = need_a | hit
            need_b[q] = need_b[q] | hit
        plan[NEED_A + p] = need_a
    for q in range(SLOTS):
        plan[NEED_B + q] = need_b[q]
    for f in range(F):
        plan[TOUCHED + f] = touched[f]


def wanted_slot(f, p, a_slots, b_slots, kept):
    v, block = a_slots[0, 0, p], kept[0, 0, f]
    wanted = jnp.where((v < 16) & ((v & 12) == (block & 12)), (v & 3) * 4 + (block & 3), -1)
    q = jnp.int32(SLOTS)
    for slot in range(SLOTS):
        q = jnp.where(b_slots[0, 0, slot] == wanted, slot, q)
    return q


def exchange_kernel(a_ref, b_ref, ai_ref, bi_ref, ci_ref, a2_ref, b2_ref, c0_ref, plan_ref, msg, got, slots, a_here, b_here,
                    c_here, l_sems, c_sems, relay, first, second,
                    a_sems, i_sems, up_send, up_recv, on_send, on_recv, b_sems, f_sems, s_sems, h_sems, m_sems, t_sems, g_sems,
                    ready):
    row, col = lax.axis_index("row"), lax.axis_index("col")
    y, z_lo = lax.rem(row, LINES), lax.div(row, LINES)
    core, chip = lax.rem(col, 2), lax.div(col, 2)
    z_hi, x = lax.rem(chip, 4), lax.div(chip, 4)
    z = z_hi * 4 + z_lo
    core0, core1 = core == 0, core == 1

    def place(px, py, pz, pcore):
        pz = lax.rem(pz, ZS)
        return (lax.rem(pz, 4) * LINES + py, (lax.rem(px, 4) * 4 + lax.div(pz, 4)) * 2 + pcore)

    def when(*conditions):
        whole = conditions[0]
        for condition in conditions[1:]:
            whole = whole & condition
        return pl.when(whole)

    def one(*conditions):
        whole = conditions[0]
        for condition in conditions[1:]:
            whole = whole & condition
        return jnp.where(whole, 1, 0)

    a_to, a_from = (row, lax.rem(col + 31, 32)), (row, lax.rem(col + 1, 32))
    relay_to = place(x, y, z + UP, 0)
    sender_z = lax.rem(z + ZS - UP, ZS)
    sender_hi = lax.div(sender_z, 4)
    sender = place(x, y, z + ZS - UP, 0)
    relay_end = place(x + jnp.where(sender_hi == 0, 3, 0), y, sender_z + 12, 1)
    last_relay = place(x + jnp.where(z_hi == 3, 1, 0), y, z + 4 + UP, 0)
    from_z = lax.rem(z + 4, ZS)

    def share(at):
        found = at * 0
        for place_z, count in enumerate(SHARE):
            if count:
                found = found + jnp.where(at == place_z, count, 0)
        return found

    my_share, relay_share, from_share = share(z), share(sender_z), share(from_z)

    sends_up, relays, gets_up = core0 & (my_share > 0), core0 & (relay_share > 0), core1 & (from_share > 0)
    up_late = z + UP < ZS
    in_late = z >= UP
    on_late = z < 4 + UP
    got_late = z >= 12 - UP
    down_late, end_late = z_hi == 0, z_hi == 3
    holds, frees = core0 & (sender_hi == 0) & TURNS, core1 & (z_hi == 0) & TURNS
    held = place(x, y, z + UP, 0)

    z_down, z_up = lax.rem(z_lo + 3, 4) * LINES, lax.rem(z_lo + 1, 4) * LINES
    here = z_lo * LINES
    top, bottom = y == 0, y == LINES - 1
    b_to = (lax.rem(row + 31, 32), col)
    b_from = (lax.rem(row + 1, 32), col)
    col0, col1 = col - core, col - core + 1

    barrier = pltpu.get_barrier_semaphore()

    def greet(device):
        pl.semaphore_signal(barrier, inc=1, device_id=device, device_id_type=MESH)

    @when(~bottom)
    def _():
        greet(b_from)

    @when(core0)
    def _():
        greet(a_from)

    @when(core1, ~end_late)
    def _():
        greet(a_from)

    @when(core0, down_late)
    def _():
        greet(a_to)

    @when(frees)
    def _():
        greet(held)

    @when(sends_up, up_late)
    def _():
        greet(relay_to)

    @when(relays, ~in_late)
    def _():
        greet(sender)

    @when(relays, on_late)
    def _():
        greet(relay_end)

    @when(gets_up, ~got_late)
    def _():
        greet(last_relay)

    @when(top)
    def _():
        for line in range(1, LINES):
            greet((here + line, col1))
        greet((z_down, col1))
        greet(b_to)

    @when(core1, ~top, ~bottom)
    def _():
        greet((z_up + y, col1))

    @when(bottom)
    def _():
        for line in range(LINES - 1):
            greet((here + line, col1))
        greet((z_up + LINES - 1, col1))

    fetch_a = pltpu.make_async_copy(a_ref, a_here, l_sems.at[0])
    fetch_b = pltpu.make_async_copy(b_ref, b_here, l_sems.at[1])
    fetch_a.start()
    fetch_b.start()

    ints = (8, 128)
    lane = lax.broadcasted_iota(jnp.int32, ints, 1)
    for which, source in enumerate((ai_ref, bi_ref)):
        packed = jnp.zeros(ints, jnp.int32)
        for slot in range(SLOTS):
            packed = jnp.where(lane == slot, source[0, 0, slot], packed)
        msg[which] = packed

    greetings = one(~top) + one(core1) + one(core0, ~down_late) + one(core1, end_late)
    greetings = greetings + one(sends_up, ~up_late) + one(relays, in_late) + one(relays, ~on_late)
    greetings = greetings + one(gets_up, got_late) + 4 * one(core1) + one(core1, ~top, ~bottom)
    greetings = greetings + one(bottom) + one(holds)
    @when(greetings > 0)
    def _():
        pl.semaphore_wait(barrier, greetings)

    def tell(which, device):
        pl.semaphore_signal(ready.at[which], inc=1, device_id=device, device_id_type=MESH)

    @when(core1, end_late)
    def _():
        tell(0, a_from)

    @when(holds)
    def _():
        tell(4, place(x, y, z + ZS - UP, 1))

    @when(core1, ~top)
    def _():
        tell(3, (here, col0))
        tell(3, (here, col1))

    @when(core1, top)
    def _():
        tell(3, (z_up, col0))
        tell(3, (z_up, col1))

    @when(bottom)
    def _():
        tell(3, b_from)

    @when(relays, in_late)
    def _():
        tell(1, sender)

    @when(gets_up, got_late)
    def _():
        tell(2, last_relay)

    def remote(src, dst, send, recv, device):
        return pltpu.make_async_remote_copy(src_ref=src, dst_ref=dst, send_sem=send, recv_sem=recv,
                                            device_id=device, device_id_type=MESH)

    def head(g):
        rows = pl.ds(0, ROWS - g * CHUNK)
        return remote(a_ref.at[rows], a2_ref.at[rows], a_sems.at[0], a_sems.at[1], a_to)

    def chunk_rows(g, n):
        return pl.ds(ROWS - g * CHUNK + n * CHUNK, CHUNK)

    def slot_rows(n):
        return pl.ds(n * CHUNK, CHUNK)

    def up(g, n):
        return remote(a_ref.at[chunk_rows(g, n)], relay.at[slot_rows(n)], up_send.at[n], up_recv.at[n], relay_to)

    def on(g, n):
        return remote(relay.at[slot_rows(n)], a2_ref.at[chunk_rows(g, n)], on_send.at[n], on_recv.at[n], relay_end)

    whole = remote(a_ref, a2_ref, a_sems.at[0], a_sems.at[1], a_to)
    ints_a = remote(msg.at[0], got.at[0], i_sems.at[0], i_sems.at[1], a_to)
    ints_b = remote(msg.at[1], got.at[1], i_sems.at[2], i_sems.at[3], b_to)
    b_main = remote(b_ref, b2_ref, b_sems.at[0], b_sems.at[1], b_to)

    def part(line):
        return pl.ds(line * PIECE, PIECE)

    my_part = pl.ds(pl.multiple_of(y * PIECE, PIECE), PIECE)

    def leg_y(line, c):
        return remote(b_ref.at[part(line)], first.at[c], f_sems.at[line], h_sems.at[c], (here + line, col1))

    def leg_z(c):
        return remote(b_ref.at[part(0)], second.at[c], f_sems.at[0], s_sems.at[c], (z_down, col1))

    def then_z(c):
        return remote(first.at[c], second.at[c], m_sems.at[c], s_sems.at[c], (z_down + y, col1))

    def then_end(c):
        return remote(first.at[c], b2_ref.at[part(LINES - 1)], m_sems.at[c], g_sems.at[LINES - 1],
                      (z_down + LINES - 1, col0 + c))

    def then_y(c):
        return remote(second.at[c], b2_ref.at[my_part], t_sems.at[c], g_sems.at[y], (here + LINES - 1, col0 + c))

    def arrival(line):
        return remote(second.at[0], b2_ref.at[part(line)], t_sems.at[0], g_sems.at[line], (here, col))

    def down():
        for g in COUNTS:
            @when(core0, ~down_late, my_share == g)
            def _():
                ints_a.start()
                if g * CHUNK < ROWS:
                    head(g).start()

    if FIRST:
        down()

    @when(core1)
    def _():
        whole.start()

    @when(~top)
    def _():
        b_main.start()
        ints_b.start()

    @when(core1)
    def _():
        ints_a.start()

    if not FIRST:
        down()

    def kept_block(f, carry):
        total = jnp.zeros((BS, BS), jnp.float32)
        for p in range(SLOTS):
            q = wanted_slot(f, p, ai_ref, bi_ref, ci_ref)
            right = jnp.zeros((BS, BS), jnp.float32)
            for slot in range(SLOTS):
                right = jnp.where(q == slot, b_here[pl.ds(slot * BS, BS), :], right)
            total = total + block_product(a_here[pl.ds(p * BS, BS), :], right)
        c_here[f] = total
        return carry

    stores = [pltpu.make_async_copy(c_here.at[f], c0_ref.at[f], c_sems.at[f]) for f in range(F)]

    def early(first_f, last_f):
        lax.fori_loop(first_f, last_f, kept_block, 0)
        for f in range(first_f, last_f):
            stores[f].start()

    fetch_a.wait()
    fetch_b.wait()
    early(0, HALF)

    for c in range(2):
        @when(top, core == c)
        def _():
            pl.semaphore_wait(ready.at[3], LINES + 1)
            for line in (4, 3, 5, 2, 6, 1, 7):
                leg_y(line, c).start()
            leg_z(c).start()
            ints_b.start()

    @when(sends_up, up_late)
    def _():
        pl.semaphore_wait(ready.at[1], 1)

    for g in COUNTS:
        if g:
            @when(core0, my_share == g)
            def _():
                for n in range(g):
                    up(g, n).start()

    @when(core0, down_late)
    def _():
        pl.semaphore_wait(ready.at[0], 1)
        ints_a.start()

    for g in COUNTS:
        if g * CHUNK < ROWS:
            @when(core0, down_late, my_share == g)
            def _():
                head(g).start()

    @when(core0)
    def _():
        early(HALF, F)

    @when(relays, on_late)
    def _():
        pl.semaphore_wait(ready.at[2], 1)

    @when(holds)
    def _():
        pl.semaphore_wait(ready.at[5], 1)

    for g in COUNTS:
        if g:
            @when(core0, relay_share == g)
            def _():
                for n in range(g):
                    up(g, n).wait_recv()
                    on(g, n).start()

    for c in range(2):
        @when(core1, ~top)
        def _():
            leg_y(1, c).wait_recv()

        @when(core1, ~top, ~bottom)
        def _():
            then_z(c).start()

        @when(core1, bottom)
        def _():
            then_end(c).start()

    @when(core1)
    def _():
        early(HALF, F)

    for c in range(2):
        @when(core1, ~bottom)
        def _():
            leg_z(c).wait_recv()
            then_y(c).start()

    for g in COUNTS:
        if g:
            @when(frees, from_share == g)
            def _():
                for n in range(g):
                    on(g, n).wait_recv()

    @when(frees)
    def _():
        pl.semaphore_wait(ready.at[4], 1)
        tell(5, held)

    ints_a.wait()
    ints_b.wait()
    fetch_slots = pltpu.make_async_copy(got, slots, l_sems.at[2])
    fetch_slots.start()
    fetch_slots.wait()
    plan_later(slots, ci_ref, plan_ref)
    for f in range(F):
        met = jnp.int32(0)
        for p in range(SLOTS):
            met = met | jnp.where(wanted_slot(f, p, ai_ref, bi_ref, ci_ref) < SLOTS, 1, 0)
        plan_ref[BEGUN + f] = met

    @when(core1)
    def _():
        whole.wait_send()

    @when(core0)
    def _():
        whole.wait_recv()

    @when(~top)
    def _():
        b_main.wait_send()

    @when(~bottom)
    def _():
        b_main.wait_recv()

    @when(top)
    def _():
        leg_z(0).wait_send()
        for line in range(1, LINES):
            leg_y(line, 0).wait_send()

    for c in range(2):
        @when(core1, ~top)
        def _():
            then_z(c).wait_send()

        @when(core1, ~bottom)
        def _():
            then_y(c).wait_send()

    @when(bottom)
    def _():
        for line in range(LINES):
            arrival(line).wait_recv()

    for g in COUNTS:
        @when(core0, my_share == g)
        def _():
            for n in range(g):
                up(g, n).wait_send()
            if g * CHUNK < ROWS:
                head(g).wait_send()

        @when(core0, relay_share == g)
        def _():
            for n in range(g):
                on(g, n).wait_send()

        @when(core1, from_share == g)
        def _():
            if g * CHUNK < ROWS:
                head(g).wait_recv()

        if g:
            @when(core1, from_share == g, ~frees)
            def _():
                for n in range(g):
                    on(g, n).wait_recv()

    for f in range(F):
        stores[f].wait()


def exchange(a, b, a_index, b_index, c_index):
    panel = jax.ShapeDtypeStruct((ROWS, BS), jnp.float32)
    blocks = jax.ShapeDtypeStruct((F, BS, BS), jnp.float32)
    plan = jax.ShapeDtypeStruct((PLAN,), jnp.int32)
    dma = pltpu.SemaphoreType.DMA
    return pl.pallas_call(
        exchange_kernel,
        out_shape=(panel, panel, blocks, plan),
        in_specs=[HBM, HBM, SMEM, SMEM, SMEM],
        out_specs=(HBM, HBM, HBM, SMEM),
        scratch_shapes=[
            pltpu.VMEM((2, 8, 128), jnp.int32),
            pltpu.VMEM((2, 8, 128), jnp.int32),
            pltpu.SMEM((2, 8, 128), jnp.int32),
            pltpu.VMEM((ROWS, BS), jnp.float32),
            pltpu.VMEM((ROWS, BS), jnp.float32),
            pltpu.VMEM((F, BS, BS), jnp.float32),
            dma((3,)),
            dma((F,)),
            pltpu.VMEM((MOST * CHUNK, BS), jnp.float32),
            pltpu.VMEM((2, PIECE, BS), jnp.float32),
            pltpu.VMEM((2, PIECE, BS), jnp.float32),
            dma((2,)),
            dma((4,)),
            dma((MOST,)),
            dma((MOST,)),
            dma((MOST,)),
            dma((MOST,)),
            dma((2,)),
            dma((LINES,)),
            dma((2,)),
            dma((2,)),
            dma((2,)),
            dma((2,)),
            dma((LINES,)),
            pltpu.SemaphoreType.REGULAR((6,)),
        ],
        compiler_params=pltpu.CompilerParams(collective_id=0, has_side_effects=True, vmem_limit_bytes=VMEM),
        cost_estimate=pl.CostEstimate(flops=6 * F * SLOTS * BS ** 3, bytes_accessed=12 * ROWS * BS * 4, transcendentals=0),
        name="exchange",
    )(a, b, a_index, b_index, c_index)


def product_kernel(c0, a1, b1, plan, out, va, vb, acc, blank, todo, a_sem, b_sem, in_sem, out_sem):
    touched = [plan[TOUCHED + f] for f in range(F)]
    need_a = [plan[NEED_A + p] for p in range(SLOTS)]
    need_b = [plan[NEED_B + q] for q in range(SLOTS)]

    def part(slot):
        return pl.ds(slot * BS, BS)

    fetches = []
    for p in range(SLOTS):
        fetches.append((need_a[p], pltpu.make_async_copy(a1.at[part(p)], va.at[p], a_sem.at[p])))
        fetches.append((need_b[p], pltpu.make_async_copy(b1.at[part(p)], vb.at[p], b_sem.at[p])))
    begun = [plan[BEGUN + f] for f in range(F)]
    for f in range(F):
        fetches.append((begun[f], pltpu.make_async_copy(c0.at[f], acc.at[f], in_sem.at[f])))
    blanks = [pltpu.make_async_copy(blank, out.at[f], out_sem.at[f]) for f in range(F)]
    writes = [pltpu.make_async_copy(acc.at[f], out.at[f], out_sem.at[f]) for f in range(F)]
    for need, copy in fetches:
        pl.when(need != 0)(copy.start)
    blank[...] = jnp.zeros((BS, BS), jnp.float32)
    for f in range(F):
        pl.when((begun[f] | touched[f]) == 0)(blanks[f].start)
    for f in range(F):
        @pl.when((begun[f] == 0) & (touched[f] != 0))
        def _():
            acc[f] = jnp.zeros((BS, BS), jnp.float32)

    count = jnp.int32(0)
    for p in range(SLOTS):
        for q in range(SLOTS):
            place = plan[p * SLOTS + q]
            todo[count] = (p * 4 + q) * 8 + place
            count = count + jnp.where(place < F, 1, 0)

    for need, copy in fetches:
        pl.when(need != 0)(copy.wait)

    def pair(t, carry):
        entry = todo[t]
        f = entry & 7
        acc[f] += block_product(va[entry >> 5], vb[(entry >> 3) & 3])
        return carry

    lax.fori_loop(0, count, pair, 0)
    for f in range(F):
        pl.when((begun[f] | touched[f]) != 0)(writes[f].start)
    for f in range(F):
        writes[f].wait()


def products(c0, a1, b1, plan):
    dma = pltpu.SemaphoreType.DMA
    return pl.pallas_call(
        product_kernel,
        out_shape=jax.ShapeDtypeStruct((F, BS, BS), jnp.float32),
        in_specs=[HBM, HBM, HBM, SMEM],
        out_specs=HBM,
        scratch_shapes=[
            pltpu.VMEM((SLOTS, BS, BS), jnp.float32),
            pltpu.VMEM((SLOTS, BS, BS), jnp.float32),
            pltpu.VMEM((F, BS, BS), jnp.float32),
            pltpu.VMEM((BS, BS), jnp.float32),
            pltpu.SMEM((SLOTS * SLOTS + 1,), jnp.int32),
            dma((SLOTS,)),
            dma((SLOTS,)),
            dma((F,)),
            dma((F,)),
        ],
        compiler_params=pltpu.CompilerParams(vmem_limit_bytes=VMEM),
        cost_estimate=pl.CostEstimate(flops=6 * BS ** 3, bytes_accessed=12 * BS * BS * 4, transcendentals=0),
        name="products",
    )(c0, a1, b1, plan)


def per_device(a_panels, a_index, b_panels, b_index, c_index):
    a0 = a_panels.reshape(ROWS, BS)
    b0 = b_panels.reshape(ROWS, BS)
    a1, b1, c0, plan = exchange(a0, b0, a_index, b_index, c_index)
    blocks = products(c0, a1, b1, plan)
    return blocks[None, None]


def solution(mesh):
    return jax.shard_map(
        per_device,
        mesh=mesh,
        in_specs=(
            P("row", "col", None, None, None),
            P("row", "col", None),
            P("row", "col", None, None, None),
            P("row", "col", None),
            P("row", "col", None),
        ),
        out_specs=P("row", "col", None, None, None),
        check_vma=False,
    )
```

```python
import jax
import jax.numpy as jnp
from jax import lax
from jax.experimental import pallas as pl
from jax.experimental.pallas import tpu as pltpu
from jax.sharding import PartitionSpec as P

BS = 256
SLOTS = 3
F = 6
ROWS = SLOTS * BS
LINES = 8
ZS = 16
CHUNK = 96
SHARE = (4, 4, 4, 4, 0, 0, 1, 2, 2, 2, 0, 2, 0, 0, 0, 0)
COUNTS = sorted(set(SHARE))
MOST = max(1, max(SHARE))
UP = 6
PIECE = ROWS // LINES
VMEM = 60 * 1024 * 1024

TOUCHED = SLOTS * SLOTS
BEGUN = TOUCHED + F
PLAN = BEGUN + F
HALF = F // 2

MESH = pl.DeviceIdType.MESH
HBM = pl.BlockSpec(memory_space=pltpu.HBM)
SMEM = pl.BlockSpec(memory_space=pltpu.SMEM)


def block_product(a, b):
    a_hi, b_hi = a.astype(jnp.bfloat16), b.astype(jnp.bfloat16)
    a_lo = (a - a_hi.astype(jnp.float32)).astype(jnp.bfloat16)
    b_lo = (b - b_hi.astype(jnp.float32)).astype(jnp.bfloat16)

    def dot(left, right):
        return jnp.dot(left, right, preferred_element_type=jnp.float32)

    return dot(a_hi, b_hi) + (dot(a_hi, b_lo) + dot(a_lo, b_hi))


def plan_later(slots, kept, plan):
    touched = [jnp.int32(0)] * F
    for p in range(SLOTS):
        v = slots[0, 0, p]
        for q in range(SLOTS):
            w = slots[1, 0, q]
            target = jnp.where((v < 16) & (w < 16) & ((v & 3) == (w >> 2)), (v & 12) + (w & 3), -1)
            place = jnp.int32(F)
            for f in range(F):
                mine = kept[0, 0, f] == target
                place = jnp.where(mine, f, place)
                touched[f] = jnp.where(mine, 1, touched[f])
            plan[p * SLOTS + q] = place
    for f in range(F):
        plan[TOUCHED + f] = touched[f]


def wanted_slot(f, p, a_slots, b_slots, kept):
    v, block = a_slots[0, 0, p], kept[0, 0, f]
    wanted = jnp.where((v < 16) & ((v & 12) == (block & 12)), (v & 3) * 4 + (block & 3), -1)
    q = jnp.int32(SLOTS)
    for slot in range(SLOTS):
        q = jnp.where(b_slots[0, 0, slot] == wanted, slot, q)
    return q


def exchange_kernel(a_ref, b_ref, ai_ref, bi_ref, ci_ref, a2_ref, b2_ref, c0_ref, plan_ref, msg, got, slots, a_here, b_here,
                    c_here, l_sems, c_sems, relay, first, second,
                    a_sems, i_sems, up_send, up_recv, on_send, on_recv, b_sems, f_sems, s_sems, h_sems, m_sems, t_sems, g_sems,
                    ready):
    row, col = lax.axis_index("row"), lax.axis_index("col")
    y, z_lo = lax.rem(row, LINES), lax.div(row, LINES)
    core, chip = lax.rem(col, 2), lax.div(col, 2)
    z_hi, x = lax.rem(chip, 4), lax.div(chip, 4)
    z = z_hi * 4 + z_lo
    core0, core1 = core == 0, core == 1

    def place(px, py, pz, pcore):
        pz = lax.rem(pz, ZS)
        return (lax.rem(pz, 4) * LINES + py, (lax.rem(px, 4) * 4 + lax.div(pz, 4)) * 2 + pcore)

    def when(*conditions):
        whole = conditions[0]
        for condition in conditions[1:]:
            whole = whole & condition
        return pl.when(whole)

    def one(*conditions):
        whole = conditions[0]
        for condition in conditions[1:]:
            whole = whole & condition
        return jnp.where(whole, 1, 0)

    a_to, a_from = (row, lax.rem(col + 31, 32)), (row, lax.rem(col + 1, 32))
    relay_to = place(x, y, z + UP, 0)
    sender_z = lax.rem(z + ZS - UP, ZS)
    sender_hi = lax.div(sender_z, 4)
    sender = place(x, y, z + ZS - UP, 0)
    relay_end = place(x + jnp.where(sender_hi == 0, 3, 0), y, sender_z + 12, 1)
    last_relay = place(x + jnp.where(z_hi == 3, 1, 0), y, z + 4 + UP, 0)
    from_z = lax.rem(z + 4, ZS)

    def share(at):
        found = at * 0
        for place_z, count in enumerate(SHARE):
            if count:
                found = found + jnp.where(at == place_z, count, 0)
        return found

    my_share, relay_share, from_share = share(z), share(sender_z), share(from_z)

    sends_up, relays, gets_up = core0 & (my_share > 0), core0 & (relay_share > 0), core1 & (from_share > 0)
    up_late = z + UP < ZS
    in_late = z >= UP
    on_late = z < 4 + UP
    got_late = z >= 12 - UP
    down_late, end_late = z_hi == 0, z_hi == 3

    z_down, z_up = lax.rem(z_lo + 3, 4) * LINES, lax.rem(z_lo + 1, 4) * LINES
    here = z_lo * LINES
    top, bottom = y == 0, y == LINES - 1
    b_to = (lax.rem(row + 31, 32), col)
    b_from = (lax.rem(row + 1, 32), col)
    col0, col1 = col - core, col - core + 1

    barrier = pltpu.get_barrier_semaphore()

    def greet(device):
        pl.semaphore_signal(barrier, inc=1, device_id=device, device_id_type=MESH)

    @when(~bottom)
    def _():
        greet(b_from)

    @when(core0)
    def _():
        greet(a_from)

    @when(core1, ~end_late)
    def _():
        greet(a_from)

    @when(core0, down_late)
    def _():
        greet(a_to)

    @when(sends_up, up_late)
    def _():
        greet(relay_to)

    @when(relays, ~in_late)
    def _():
        greet(sender)

    @when(relays, on_late)
    def _():
        greet(relay_end)

    @when(gets_up, ~got_late)
    def _():
        greet(last_relay)

    @when(top)
    def _():
        for line in range(1, LINES):
            greet((here + line, col1))
        greet((z_down, col1))
        greet(b_to)

    @when(core1, ~top, ~bottom)
    def _():
        greet((z_up + y, col1))

    @when(bottom)
    def _():
        for line in range(LINES - 1):
            greet((here + line, col1))
        greet((z_up + LINES - 1, col1))

    fetch_a = pltpu.make_async_copy(a_ref, a_here, l_sems.at[0])
    fetch_b = pltpu.make_async_copy(b_ref, b_here, l_sems.at[1])
    fetch_a.start()
    fetch_b.start()

    ints = (8, 128)
    lane = lax.broadcasted_iota(jnp.int32, ints, 1)
    for which, source in enumerate((ai_ref, bi_ref)):
        packed = jnp.zeros(ints, jnp.int32)
        for slot in range(SLOTS):
            packed = jnp.where(lane == slot, source[0, 0, slot], packed)
        msg[which] = packed

    greetings = one(~top) + one(core1) + one(core0, ~down_late) + one(core1, end_late)
    greetings = greetings + one(sends_up, ~up_late) + one(relays, in_late) + one(relays, ~on_late)
    greetings = greetings + one(gets_up, got_late) + 4 * one(core1) + one(core1, ~top, ~bottom)
    greetings = greetings + one(bottom)
    @when(greetings > 0)
    def _():
        pl.semaphore_wait(barrier, greetings)

    def tell(which, device):
        pl.semaphore_signal(ready.at[which], inc=1, device_id=device, device_id_type=MESH)

    @when(core1, end_late)
    def _():
        tell(0, a_from)

    @when(core1, ~top)
    def _():
        tell(3, (here, col0))
        tell(3, (here, col1))

    @when(core1, top)
    def _():
        tell(3, (z_up, col0))
        tell(3, (z_up, col1))

    @when(bottom)
    def _():
        tell(3, b_from)

    @when(relays, in_late)
    def _():
        tell(1, sender)

    @when(gets_up, got_late)
    def _():
        tell(2, last_relay)

    def remote(src, dst, send, recv, device):
        return pltpu.make_async_remote_copy(src_ref=src, dst_ref=dst, send_sem=send, recv_sem=recv,
                                            device_id=device, device_id_type=MESH)

    def head(g):
        rows = pl.ds(0, ROWS - g * CHUNK)
        return remote(a_ref.at[rows], a2_ref.at[rows], a_sems.at[0], a_sems.at[1], a_to)

    def chunk_rows(g, n):
        return pl.ds(ROWS - g * CHUNK + n * CHUNK, CHUNK)

    def slot_rows(n):
        return pl.ds(n * CHUNK, CHUNK)

    def up(g, n):
        return remote(a_ref.at[chunk_rows(g, n)], relay.at[slot_rows(n)], up_send.at[n], up_recv.at[n], relay_to)

    def on(g, n):
        return remote(relay.at[slot_rows(n)], a2_ref.at[chunk_rows(g, n)], on_send.at[n], on_recv.at[n], relay_end)

    whole = remote(a_ref, a2_ref, a_sems.at[0], a_sems.at[1], a_to)
    ints_a = remote(msg.at[0], got.at[0], i_sems.at[0], i_sems.at[1], a_to)
    ints_b = remote(msg.at[1], got.at[1], i_sems.at[2], i_sems.at[3], b_to)
    b_main = remote(b_ref, b2_ref, b_sems.at[0], b_sems.at[1], b_to)

    def part(line):
        return pl.ds(line * PIECE, PIECE)

    my_part = pl.ds(pl.multiple_of(y * PIECE, PIECE), PIECE)

    def leg_y(line, c):
        return remote(b_ref.at[part(line)], first.at[c], f_sems.at[line], h_sems.at[c], (here + line, col1))

    def leg_z(c):
        return remote(b_ref.at[part(0)], second.at[c], f_sems.at[0], s_sems.at[c], (z_down, col1))

    def then_z(c):
        return remote(first.at[c], second.at[c], m_sems.at[c], s_sems.at[c], (z_down + y, col1))

    def then_end(c):
        return remote(first.at[c], b2_ref.at[part(LINES - 1)], m_sems.at[c], g_sems.at[LINES - 1],
                      (z_down + LINES - 1, col0 + c))

    def then_y(c):
        return remote(second.at[c], b2_ref.at[my_part], t_sems.at[c], g_sems.at[y], (here + LINES - 1, col0 + c))

    def arrival(line):
        return remote(second.at[0], b2_ref.at[part(line)], t_sems.at[0], g_sems.at[line], (here, col))

    @when(core1)
    def _():
        whole.start()

    @when(~top)
    def _():
        b_main.start()
        ints_b.start()

    @when(core1)
    def _():
        ints_a.start()

    for g in COUNTS:
        @when(core0, ~down_late, my_share == g)
        def _():
            ints_a.start()
            if g * CHUNK < ROWS:
                head(g).start()

    def kept_block(f, carry):
        total = jnp.zeros((BS, BS), jnp.float32)
        for p in range(SLOTS):
            q = wanted_slot(f, p, ai_ref, bi_ref, ci_ref)
            right = jnp.zeros((BS, BS), jnp.float32)
            for slot in range(SLOTS):
                right = jnp.where(q == slot, b_here[pl.ds(slot * BS, BS), :], right)
            total = total + block_product(a_here[pl.ds(p * BS, BS), :], right)
        c_here[f] = total
        return carry

    stores = [pltpu.make_async_copy(c_here.at[f], c0_ref.at[f], c_sems.at[f]) for f in range(F)]

    def early(first_f, last_f):
        lax.fori_loop(first_f, last_f, kept_block, 0)
        for f in range(first_f, last_f):
            stores[f].start()

    fetch_a.wait()
    fetch_b.wait()
    early(0, HALF)

    for c in range(2):
        @when(top, core == c)
        def _():
            pl.semaphore_wait(ready.at[3], LINES + 1)
            for line in (4, 3, 5, 2, 6, 1, 7):
                leg_y(line, c).start()
            leg_z(c).start()
            ints_b.start()

    @when(sends_up, up_late)
    def _():
        pl.semaphore_wait(ready.at[1], 1)

    for g in COUNTS:
        if g:
            @when(core0, my_share == g)
            def _():
                for n in range(g):
                    up(g, n).start()

    @when(core0, down_late)
    def _():
        pl.semaphore_wait(ready.at[0], 1)
        ints_a.start()

    for g in COUNTS:
        if g * CHUNK < ROWS:
            @when(core0, down_late, my_share == g)
            def _():
                head(g).start()

    @when(core0)
    def _():
        early(HALF, F)

    @when(relays, on_late)
    def _():
        pl.semaphore_wait(ready.at[2], 1)

    for g in COUNTS:
        if g:
            @when(core0, relay_share == g)
            def _():
                for n in range(g):
                    up(g, n).wait_recv()
                    on(g, n).start()

    for c in range(2):
        @when(core1, ~top)
        def _():
            leg_y(1, c).wait_recv()

        @when(core1, ~top, ~bottom)
        def _():
            then_z(c).start()

        @when(core1, bottom)
        def _():
            then_end(c).start()

    @when(core1)
    def _():
        early(HALF, F)

    for c in range(2):
        @when(core1, ~bottom)
        def _():
            leg_z(c).wait_recv()
            then_y(c).start()

    ints_a.wait()
    ints_b.wait()
    fetch_slots = pltpu.make_async_copy(got, slots, l_sems.at[2])
    fetch_slots.start()
    fetch_slots.wait()
    plan_later(slots, ci_ref, plan_ref)
    for f in range(F):
        met = jnp.int32(0)
        for p in range(SLOTS):
            met = met | jnp.where(wanted_slot(f, p, ai_ref, bi_ref, ci_ref) < SLOTS, 1, 0)
        plan_ref[BEGUN + f] = met

    @when(core1)
    def _():
        whole.wait_send()

    @when(core0)
    def _():
        whole.wait_recv()

    @when(~top)
    def _():
        b_main.wait_send()

    @when(~bottom)
    def _():
        b_main.wait_recv()

    @when(top)
    def _():
        leg_z(0).wait_send()
        for line in range(1, LINES):
            leg_y(line, 0).wait_send()

    for c in range(2):
        @when(core1, ~top)
        def _():
            then_z(c).wait_send()

        @when(core1, ~bottom)
        def _():
            then_y(c).wait_send()

    @when(bottom)
    def _():
        for line in range(LINES):
            arrival(line).wait_recv()

    for g in COUNTS:
        @when(core0, my_share == g)
        def _():
            for n in range(g):
                up(g, n).wait_send()
            if g * CHUNK < ROWS:
                head(g).wait_send()

        @when(core0, relay_share == g)
        def _():
            for n in range(g):
                on(g, n).wait_send()

        @when(core1, from_share == g)
        def _():
            if g * CHUNK < ROWS:
                head(g).wait_recv()

        if g:
            @when(core1, from_share == g)
            def _():
                for n in range(g):
                    on(g, n).wait_recv()

    for f in range(F):
        stores[f].wait()


def exchange(a, b, a_index, b_index, c_index):
    panel = jax.ShapeDtypeStruct((ROWS, BS), jnp.float32)
    blocks = jax.ShapeDtypeStruct((F, BS, BS), jnp.float32)
    plan = jax.ShapeDtypeStruct((PLAN,), jnp.int32)
    dma = pltpu.SemaphoreType.DMA
    return pl.pallas_call(
        exchange_kernel,
        out_shape=(panel, panel, blocks, plan),
        in_specs=[HBM, HBM, SMEM, SMEM, SMEM],
        out_specs=(HBM, HBM, HBM, SMEM),
        scratch_shapes=[
            pltpu.VMEM((2, 8, 128), jnp.int32),
            pltpu.VMEM((2, 8, 128), jnp.int32),
            pltpu.SMEM((2, 8, 128), jnp.int32),
            pltpu.VMEM((ROWS, BS), jnp.float32),
            pltpu.VMEM((ROWS, BS), jnp.float32),
            pltpu.VMEM((F, BS, BS), jnp.float32),
            dma((3,)),
            dma((F,)),
            pltpu.VMEM((MOST * CHUNK, BS), jnp.float32),
            pltpu.VMEM((2, PIECE, BS), jnp.float32),
            pltpu.VMEM((2, PIECE, BS), jnp.float32),
            dma((2,)),
            dma((4,)),
            dma((MOST,)),
            dma((MOST,)),
            dma((MOST,)),
            dma((MOST,)),
            dma((2,)),
            dma((LINES,)),
            dma((2,)),
            dma((2,)),
            dma((2,)),
            dma((2,)),
            dma((LINES,)),
            pltpu.SemaphoreType.REGULAR((4,)),
        ],
        compiler_params=pltpu.CompilerParams(collective_id=0, has_side_effects=True, vmem_limit_bytes=VMEM),
        cost_estimate=pl.CostEstimate(flops=6 * F * SLOTS * BS ** 3, bytes_accessed=12 * ROWS * BS * 4, transcendentals=0),
        name="exchange",
    )(a, b, a_index, b_index, c_index)


def product_kernel(c0, a1, b1, plan_ref, out, plan, va, vb, acc, blank, todo, p_sem, a_sem, b_sem, in_sem, out_sem):
    fetch_plan = pltpu.make_async_copy(plan_ref, plan, p_sem)
    fetch_plan.start()
    fetches = [pltpu.make_async_copy(a1, va, a_sem), pltpu.make_async_copy(b1, vb, b_sem)]
    for copy in fetches:
        copy.start()
    blank[...] = jnp.zeros((BS, BS), jnp.float32)
    fetch_plan.wait()
    touched = [plan[TOUCHED + f] for f in range(F)]
    begun = [plan[BEGUN + f] for f in range(F)]
    starts = [pltpu.make_async_copy(c0.at[f], acc.at[f], in_sem.at[f]) for f in range(F)]
    blanks = [pltpu.make_async_copy(blank, out.at[f], out_sem.at[f]) for f in range(F)]
    writes = [pltpu.make_async_copy(acc.at[f], out.at[f], out_sem.at[f]) for f in range(F)]
    for f in range(F):
        pl.when(begun[f] != 0)(starts[f].start)
    for f in range(F):
        pl.when((begun[f] | touched[f]) == 0)(blanks[f].start)
    for f in range(F):
        @pl.when((begun[f] == 0) & (touched[f] != 0))
        def _():
            acc[f] = jnp.zeros((BS, BS), jnp.float32)

    count = jnp.int32(0)
    for p in range(SLOTS):
        for q in range(SLOTS):
            place = plan[p * SLOTS + q]
            todo[count] = (p * 4 + q) * 8 + place
            count = count + jnp.where(place < F, 1, 0)

    for f in range(F):
        pl.when(begun[f] != 0)(starts[f].wait)
    for f in range(F):
        pl.when((begun[f] != 0) & (touched[f] == 0))(writes[f].start)
    for copy in fetches:
        copy.wait()

    def pair(t, carry):
        entry = todo[t]
        f = entry & 7
        left = va[pl.ds(pl.multiple_of((entry >> 5) * BS, BS), BS), :]
        right = vb[pl.ds(pl.multiple_of(((entry >> 3) & 3) * BS, BS), BS), :]
        acc[f] += block_product(left, right)
        return carry

    lax.fori_loop(0, count, pair, 0)
    for f in range(F):
        pl.when(touched[f] != 0)(writes[f].start)
    for f in range(F):
        writes[f].wait()


def products(c0, a1, b1, plan):
    dma = pltpu.SemaphoreType.DMA
    return pl.pallas_call(
        product_kernel,
        out_shape=jax.ShapeDtypeStruct((F, BS, BS), jnp.float32),
        in_specs=[HBM, HBM, HBM, HBM],
        out_specs=HBM,
        scratch_shapes=[
            pltpu.SMEM((PLAN,), jnp.int32),
            pltpu.VMEM((ROWS, BS), jnp.float32),
            pltpu.VMEM((ROWS, BS), jnp.float32),
            pltpu.VMEM((F, BS, BS), jnp.float32),
            pltpu.VMEM((BS, BS), jnp.float32),
            pltpu.SMEM((SLOTS * SLOTS + 1,), jnp.int32),
            dma,
            dma,
            dma,
            dma((F,)),
            dma((F,)),
        ],
        compiler_params=pltpu.CompilerParams(vmem_limit_bytes=VMEM),
        cost_estimate=pl.CostEstimate(flops=6 * BS ** 3, bytes_accessed=12 * BS * BS * 4, transcendentals=0),
        name="products",
    )(c0, a1, b1, plan)


def per_device(a_panels, a_index, b_panels, b_index, c_index):
    a0 = a_panels.reshape(ROWS, BS)
    b0 = b_panels.reshape(ROWS, BS)
    a1, b1, c0, plan = exchange(a0, b0, a_index, b_index, c_index)
    blocks = products(c0, a1, b1, plan)
    return blocks[None, None]


def solution(mesh):
    return jax.shard_map(
        per_device,
        mesh=mesh,
        in_specs=(
            P("row", "col", None, None, None),
            P("row", "col", None),
            P("row", "col", None, None, None),
            P("row", "col", None),
            P("row", "col", None),
        ),
        out_specs=P("row", "col", None, None, None),
        check_vma=False,
    )
```

```python
import jax
import jax.numpy as jnp
from jax import lax
from jax.experimental import pallas as pl
from jax.experimental.pallas import tpu as pltpu
from jax.sharding import PartitionSpec as P

BS = 256
SLOTS = 3
F = 6
ROWS = SLOTS * BS
LINES = 8
ZS = 16
CHUNK = 96
SHARE = (4, 4, 4, 4, 0, 0, 1, 2, 2, 2, 0, 2, 0, 0, 0, 0)
COUNTS = sorted(set(SHARE))
MOST = max(1, max(SHARE))
UP = 6
PIECE = ROWS // LINES
VMEM = 60 * 1024 * 1024

TOUCHED = SLOTS * SLOTS
PLAN = TOUCHED + F
HALF = F // 2

MESH = pl.DeviceIdType.MESH
HBM = pl.BlockSpec(memory_space=pltpu.HBM)
SMEM = pl.BlockSpec(memory_space=pltpu.SMEM)


def block_product(a, b):
    a_hi, b_hi = a.astype(jnp.bfloat16), b.astype(jnp.bfloat16)
    a_lo = (a - a_hi.astype(jnp.float32)).astype(jnp.bfloat16)
    b_lo = (b - b_hi.astype(jnp.float32)).astype(jnp.bfloat16)

    def dot(left, right):
        return jnp.dot(left, right, preferred_element_type=jnp.float32)

    return dot(a_hi, b_hi) + (dot(a_hi, b_lo) + dot(a_lo, b_hi))


def plan_later(slots, kept, plan):
    touched = [jnp.int32(0)] * F
    for p in range(SLOTS):
        v = slots[0, 0, p]
        for q in range(SLOTS):
            w = slots[1, 0, q]
            target = jnp.where((v < 16) & (w < 16) & ((v & 3) == (w >> 2)), (v & 12) + (w & 3), -1)
            place = jnp.int32(F)
            for f in range(F):
                mine = kept[0, 0, f] == target
                place = jnp.where(mine, f, place)
                touched[f] = jnp.where(mine, 1, touched[f])
            plan[p * SLOTS + q] = place
    for f in range(F):
        plan[TOUCHED + f] = touched[f]


def wanted_slot(f, p, a_slots, b_slots, kept):
    v, block = a_slots[0, 0, p], kept[0, 0, f]
    wanted = jnp.where((v < 16) & ((v & 12) == (block & 12)), (v & 3) * 4 + (block & 3), -1)
    q = jnp.int32(SLOTS)
    for slot in range(SLOTS):
        q = jnp.where(b_slots[0, 0, slot] == wanted, slot, q)
    return q


def exchange_kernel(a_ref, b_ref, ai_ref, bi_ref, ci_ref, a2_ref, b2_ref, c0_ref, plan_ref, msg, got, slots, a_here, b_here,
                    c_here, l_sems, c_sems, relay, first, second,
                    a_sems, i_sems, up_send, up_recv, on_send, on_recv, b_sems, f_sems, s_sems, h_sems, m_sems, t_sems, g_sems,
                    ready):
    row, col = lax.axis_index("row"), lax.axis_index("col")
    y, z_lo = lax.rem(row, LINES), lax.div(row, LINES)
    core, chip = lax.rem(col, 2), lax.div(col, 2)
    z_hi, x = lax.rem(chip, 4), lax.div(chip, 4)
    z = z_hi * 4 + z_lo
    core0, core1 = core == 0, core == 1

    def place(px, py, pz, pcore):
        pz = lax.rem(pz, ZS)
        return (lax.rem(pz, 4) * LINES + py, (lax.rem(px, 4) * 4 + lax.div(pz, 4)) * 2 + pcore)

    def when(*conditions):
        whole = conditions[0]
        for condition in conditions[1:]:
            whole = whole & condition
        return pl.when(whole)

    def one(*conditions):
        whole = conditions[0]
        for condition in conditions[1:]:
            whole = whole & condition
        return jnp.where(whole, 1, 0)

    a_to, a_from = (row, lax.rem(col + 31, 32)), (row, lax.rem(col + 1, 32))
    relay_to = place(x, y, z + UP, 0)
    sender_z = lax.rem(z + ZS - UP, ZS)
    sender_hi = lax.div(sender_z, 4)
    sender = place(x, y, z + ZS - UP, 0)
    relay_end = place(x + jnp.where(sender_hi == 0, 3, 0), y, sender_z + 12, 1)
    last_relay = place(x + jnp.where(z_hi == 3, 1, 0), y, z + 4 + UP, 0)
    from_z = lax.rem(z + 4, ZS)

    def share(at):
        found = at * 0
        for place_z, count in enumerate(SHARE):
            if count:
                found = found + jnp.where(at == place_z, count, 0)
        return found

    my_share, relay_share, from_share = share(z), share(sender_z), share(from_z)

    sends_up, relays, gets_up = core0 & (my_share > 0), core0 & (relay_share > 0), core1 & (from_share > 0)
    up_late = z + UP < ZS
    in_late = z >= UP
    on_late = z < 4 + UP
    got_late = z >= 12 - UP
    down_late, end_late = z_hi == 0, z_hi == 3

    z_down, z_up = lax.rem(z_lo + 3, 4) * LINES, lax.rem(z_lo + 1, 4) * LINES
    here = z_lo * LINES
    top, bottom = y == 0, y == LINES - 1
    b_to = (lax.rem(row + 31, 32), col)
    b_from = (lax.rem(row + 1, 32), col)
    col0, col1 = col - core, col - core + 1

    barrier = pltpu.get_barrier_semaphore()

    def greet(device):
        pl.semaphore_signal(barrier, inc=1, device_id=device, device_id_type=MESH)

    @when(~bottom)
    def _():
        greet(b_from)

    @when(core0)
    def _():
        greet(a_from)

    @when(core1, ~end_late)
    def _():
        greet(a_from)

    @when(core0, down_late)
    def _():
        greet(a_to)

    @when(sends_up, up_late)
    def _():
        greet(relay_to)

    @when(relays, ~in_late)
    def _():
        greet(sender)

    @when(relays, on_late)
    def _():
        greet(relay_end)

    @when(gets_up, ~got_late)
    def _():
        greet(last_relay)

    @when(top)
    def _():
        for line in range(1, LINES):
            greet((here + line, col1))
        greet((z_down, col1))
        greet(b_to)

    @when(core1, ~top, ~bottom)
    def _():
        greet((z_up + y, col1))

    @when(bottom)
    def _():
        for line in range(LINES - 1):
            greet((here + line, col1))
        greet((z_up + LINES - 1, col1))

    fetch_a = pltpu.make_async_copy(a_ref, a_here, l_sems.at[0])
    fetch_b = pltpu.make_async_copy(b_ref, b_here, l_sems.at[1])
    fetch_a.start()
    fetch_b.start()

    ints = (8, 128)
    lane = lax.broadcasted_iota(jnp.int32, ints, 1)
    for which, source in enumerate((ai_ref, bi_ref)):
        packed = jnp.zeros(ints, jnp.int32)
        for slot in range(SLOTS):
            packed = jnp.where(lane == slot, source[0, 0, slot], packed)
        msg[which] = packed

    greetings = one(~top) + one(core1) + one(core0, ~down_late) + one(core1, end_late)
    greetings = greetings + one(sends_up, ~up_late) + one(relays, in_late) + one(relays, ~on_late)
    greetings = greetings + one(gets_up, got_late) + 4 * one(core1) + one(core1, ~top, ~bottom)
    greetings = greetings + one(bottom)
    @when(greetings > 0)
    def _():
        pl.semaphore_wait(barrier, greetings)

    def tell(which, device):
        pl.semaphore_signal(ready.at[which], inc=1, device_id=device, device_id_type=MESH)

    @when(core1, end_late)
    def _():
        tell(0, a_from)

    @when(core1, ~top)
    def _():
        tell(3, (here, col0))
        tell(3, (here, col1))

    @when(core1, top)
    def _():
        tell(3, (z_up, col0))
        tell(3, (z_up, col1))

    @when(bottom)
    def _():
        tell(3, b_from)

    @when(relays, in_late)
    def _():
        tell(1, sender)

    @when(gets_up, got_late)
    def _():
        tell(2, last_relay)

    def remote(src, dst, send, recv, device):
        return pltpu.make_async_remote_copy(src_ref=src, dst_ref=dst, send_sem=send, recv_sem=recv,
                                            device_id=device, device_id_type=MESH)

    def head(g):
        rows = pl.ds(0, ROWS - g * CHUNK)
        return remote(a_ref.at[rows], a2_ref.at[rows], a_sems.at[0], a_sems.at[1], a_to)

    def chunk_rows(g, n):
        return pl.ds(ROWS - g * CHUNK + n * CHUNK, CHUNK)

    def slot_rows(n):
        return pl.ds(n * CHUNK, CHUNK)

    def up(g, n):
        return remote(a_ref.at[chunk_rows(g, n)], relay.at[slot_rows(n)], up_send.at[n], up_recv.at[n], relay_to)

    def on(g, n):
        return remote(relay.at[slot_rows(n)], a2_ref.at[chunk_rows(g, n)], on_send.at[n], on_recv.at[n], relay_end)

    whole = remote(a_ref, a2_ref, a_sems.at[0], a_sems.at[1], a_to)
    ints_a = remote(msg.at[0], got.at[0], i_sems.at[0], i_sems.at[1], a_to)
    ints_b = remote(msg.at[1], got.at[1], i_sems.at[2], i_sems.at[3], b_to)
    b_main = remote(b_ref, b2_ref, b_sems.at[0], b_sems.at[1], b_to)

    def part(line):
        return pl.ds(line * PIECE, PIECE)

    my_part = pl.ds(pl.multiple_of(y * PIECE, PIECE), PIECE)

    def leg_y(line, c):
        return remote(b_ref.at[part(line)], first.at[c], f_sems.at[line], h_sems.at[c], (here + line, col1))

    def leg_z(c):
        return remote(b_ref.at[part(0)], second.at[c], f_sems.at[0], s_sems.at[c], (z_down, col1))

    def then_z(c):
        return remote(first.at[c], second.at[c], m_sems.at[c], s_sems.at[c], (z_down + y, col1))

    def then_end(c):
        return remote(first.at[c], b2_ref.at[part(LINES - 1)], m_sems.at[c], g_sems.at[LINES - 1],
                      (z_down + LINES - 1, col0 + c))

    def then_y(c):
        return remote(second.at[c], b2_ref.at[my_part], t_sems.at[c], g_sems.at[y], (here + LINES - 1, col0 + c))

    def arrival(line):
        return remote(second.at[0], b2_ref.at[part(line)], t_sems.at[0], g_sems.at[line], (here, col))

    @when(core1)
    def _():
        whole.start()

    @when(~top)
    def _():
        b_main.start()
        ints_b.start()

    @when(core1)
    def _():
        ints_a.start()

    for g in COUNTS:
        @when(core0, ~down_late, my_share == g)
        def _():
            ints_a.start()
            if g * CHUNK < ROWS:
                head(g).start()

    def kept_block(f, carry):
        total = jnp.zeros((BS, BS), jnp.float32)
        for p in range(SLOTS):
            q = wanted_slot(f, p, ai_ref, bi_ref, ci_ref)
            right = jnp.zeros((BS, BS), jnp.float32)
            for slot in range(SLOTS):
                right = jnp.where(q == slot, b_here[pl.ds(slot * BS, BS), :], right)
            total = total + block_product(a_here[pl.ds(p * BS, BS), :], right)
        c_here[f] = total
        return carry

    stores = [pltpu.make_async_copy(c_here.at[f], c0_ref.at[f], c_sems.at[f]) for f in range(F)]

    def early(first_f, last_f):
        lax.fori_loop(first_f, last_f, kept_block, 0)
        for f in range(first_f, last_f):
            stores[f].start()

    fetch_a.wait()
    fetch_b.wait()
    early(0, HALF)

    for c in range(2):
        @when(top, core == c)
        def _():
            pl.semaphore_wait(ready.at[3], LINES + 1)
            for line in (4, 3, 5, 2, 6, 1, 7):
                leg_y(line, c).start()
            leg_z(c).start()
            ints_b.start()

    @when(sends_up, up_late)
    def _():
        pl.semaphore_wait(ready.at[1], 1)

    for g in COUNTS:
        if g:
            @when(core0, my_share == g)
            def _():
                for n in range(g):
                    up(g, n).start()

    @when(core0, down_late)
    def _():
        pl.semaphore_wait(ready.at[0], 1)
        ints_a.start()

    for g in COUNTS:
        if g * CHUNK < ROWS:
            @when(core0, down_late, my_share == g)
            def _():
                head(g).start()

    @when(core0)
    def _():
        early(HALF, F)

    @when(relays, on_late)
    def _():
        pl.semaphore_wait(ready.at[2], 1)

    for g in COUNTS:
        if g:
            @when(core0, relay_share == g)
            def _():
                for n in range(g):
                    up(g, n).wait_recv()
                    on(g, n).start()

    for c in range(2):
        @when(core1, ~top)
        def _():
            leg_y(1, c).wait_recv()

        @when(core1, ~top, ~bottom)
        def _():
            then_z(c).start()

        @when(core1, bottom)
        def _():
            then_end(c).start()

    @when(core1)
    def _():
        early(HALF, F)

    for c in range(2):
        @when(core1, ~bottom)
        def _():
            leg_z(c).wait_recv()
            then_y(c).start()

    ints_a.wait()
    ints_b.wait()
    fetch_slots = pltpu.make_async_copy(got, slots, l_sems.at[2])
    fetch_slots.start()
    fetch_slots.wait()
    plan_later(slots, ci_ref, plan_ref)

    @when(core1)
    def _():
        whole.wait_send()

    @when(core0)
    def _():
        whole.wait_recv()

    @when(~top)
    def _():
        b_main.wait_send()

    @when(~bottom)
    def _():
        b_main.wait_recv()

    @when(top)
    def _():
        leg_z(0).wait_send()
        for line in range(1, LINES):
            leg_y(line, 0).wait_send()

    for c in range(2):
        @when(core1, ~top)
        def _():
            then_z(c).wait_send()

        @when(core1, ~bottom)
        def _():
            then_y(c).wait_send()

    @when(bottom)
    def _():
        for line in range(LINES):
            arrival(line).wait_recv()

    for g in COUNTS:
        @when(core0, my_share == g)
        def _():
            for n in range(g):
                up(g, n).wait_send()
            if g * CHUNK < ROWS:
                head(g).wait_send()

        @when(core0, relay_share == g)
        def _():
            for n in range(g):
                on(g, n).wait_send()

        @when(core1, from_share == g)
        def _():
            if g * CHUNK < ROWS:
                head(g).wait_recv()

        if g:
            @when(core1, from_share == g)
            def _():
                for n in range(g):
                    on(g, n).wait_recv()

    for f in range(F):
        stores[f].wait()


def exchange(a, b, a_index, b_index, c_index):
    panel = jax.ShapeDtypeStruct((ROWS, BS), jnp.float32)
    blocks = jax.ShapeDtypeStruct((F, BS, BS), jnp.float32)
    plan = jax.ShapeDtypeStruct((PLAN,), jnp.int32)
    dma = pltpu.SemaphoreType.DMA
    return pl.pallas_call(
        exchange_kernel,
        out_shape=(panel, panel, blocks, plan),
        in_specs=[HBM, HBM, SMEM, SMEM, SMEM],
        out_specs=(HBM, HBM, HBM, SMEM),
        scratch_shapes=[
            pltpu.VMEM((2, 8, 128), jnp.int32),
            pltpu.VMEM((2, 8, 128), jnp.int32),
            pltpu.SMEM((2, 8, 128), jnp.int32),
            pltpu.VMEM((ROWS, BS), jnp.float32),
            pltpu.VMEM((ROWS, BS), jnp.float32),
            pltpu.VMEM((F, BS, BS), jnp.float32),
            dma((3,)),
            dma((F,)),
            pltpu.VMEM((MOST * CHUNK, BS), jnp.float32),
            pltpu.VMEM((2, PIECE, BS), jnp.float32),
            pltpu.VMEM((2, PIECE, BS), jnp.float32),
            dma((2,)),
            dma((4,)),
            dma((MOST,)),
            dma((MOST,)),
            dma((MOST,)),
            dma((MOST,)),
            dma((2,)),
            dma((LINES,)),
            dma((2,)),
            dma((2,)),
            dma((2,)),
            dma((2,)),
            dma((LINES,)),
            pltpu.SemaphoreType.REGULAR((4,)),
        ],
        compiler_params=pltpu.CompilerParams(collective_id=0, has_side_effects=True, vmem_limit_bytes=VMEM),
        cost_estimate=pl.CostEstimate(flops=6 * F * SLOTS * BS ** 3, bytes_accessed=12 * ROWS * BS * 4, transcendentals=0),
        name="exchange",
    )(a, b, a_index, b_index, c_index)


def product_kernel(c0, a1, b1, plan_ref, out, plan, va, vb, acc, todo, p_sem, a_sem, b_sem, in_sem, out_sem):
    fetch_plan = pltpu.make_async_copy(plan_ref, plan, p_sem)
    fetch_plan.start()
    starts = [pltpu.make_async_copy(c0.at[f], acc.at[f], in_sem.at[f]) for f in range(F)]
    writes = [pltpu.make_async_copy(acc.at[f], out.at[f], out_sem.at[f]) for f in range(F)]
    fetches = [pltpu.make_async_copy(a1, va, a_sem), pltpu.make_async_copy(b1, vb, b_sem)]
    for copy in starts + fetches:
        copy.start()
    fetch_plan.wait()
    touched = [plan[TOUCHED + f] for f in range(F)]
    count = jnp.int32(0)
    for p in range(SLOTS):
        for q in range(SLOTS):
            place = plan[p * SLOTS + q]
            todo[count] = (p * 4 + q) * 8 + place
            count = count + jnp.where(place < F, 1, 0)

    for f in range(F):
        starts[f].wait()
        pl.when(touched[f] == 0)(writes[f].start)
    for copy in fetches:
        copy.wait()

    def pair(t, carry):
        entry = todo[t]
        f = entry & 7
        left = va[pl.ds(pl.multiple_of((entry >> 5) * BS, BS), BS), :]
        right = vb[pl.ds(pl.multiple_of(((entry >> 3) & 3) * BS, BS), BS), :]
        acc[f] += block_product(left, right)
        return carry

    lax.fori_loop(0, count, pair, 0)
    for f in range(F):
        pl.when(touched[f] != 0)(writes[f].start)
    for f in range(F):
        writes[f].wait()


def products(c0, a1, b1, plan):
    dma = pltpu.SemaphoreType.DMA
    return pl.pallas_call(
        product_kernel,
        out_shape=jax.ShapeDtypeStruct((F, BS, BS), jnp.float32),
        in_specs=[HBM, HBM, HBM, HBM],
        out_specs=HBM,
        scratch_shapes=[
            pltpu.SMEM((PLAN,), jnp.int32),
            pltpu.VMEM((ROWS, BS), jnp.float32),
            pltpu.VMEM((ROWS, BS), jnp.float32),
            pltpu.VMEM((F, BS, BS), jnp.float32),
            pltpu.SMEM((SLOTS * SLOTS + 1,), jnp.int32),
            dma,
            dma,
            dma,
            dma((F,)),
            dma((F,)),
        ],
        compiler_params=pltpu.CompilerParams(vmem_limit_bytes=VMEM),
        cost_estimate=pl.CostEstimate(flops=6 * BS ** 3, bytes_accessed=12 * BS * BS * 4, transcendentals=0),
        name="products",
    )(c0, a1, b1, plan)


def per_device(a_panels, a_index, b_panels, b_index, c_index):
    a0 = a_panels.reshape(ROWS, BS)
    b0 = b_panels.reshape(ROWS, BS)
    a1, b1, c0, plan = exchange(a0, b0, a_index, b_index, c_index)
    blocks = products(c0, a1, b1, plan)
    return blocks[None, None]


def solution(mesh):
    return jax.shard_map(
        per_device,
        mesh=mesh,
        in_specs=(
            P("row", "col", None, None, None),
            P("row", "col", None),
            P("row", "col", None, None, None),
            P("row", "col", None),
            P("row", "col", None),
        ),
        out_specs=P("row", "col", None, None, None),
        check_vma=False,
    )
```

```python
import jax
import jax.numpy as jnp
from jax import lax
from jax.experimental import pallas as pl
from jax.experimental.pallas import tpu as pltpu
from jax.sharding import PartitionSpec as P

BS = 256
SLOTS = 3
F = 6
ROWS = SLOTS * BS
LINES = 8
ZS = 16
CHUNK = 96
SHARE = (4, 4, 4, 4, 0, 0, 1, 2, 2, 2, 0, 2, 0, 0, 0, 0)
SIDE = (0, 0, 0, 0, 6, 2, 0, 0, 0, 0, 0, 0, 0, 0, 0, 0)
COUNTS = sorted(set(SHARE))
PAIRS = sorted(set(zip(SHARE, SIDE)))
ALL = ROWS // CHUNK
MOST = max(1, max(SHARE))
UP = 6
PIECE = ROWS // LINES
VMEM = 60 * 1024 * 1024

TOUCHED = SLOTS * SLOTS
PLAN = TOUCHED + F
HALF = 0

MESH = pl.DeviceIdType.MESH
HBM = pl.BlockSpec(memory_space=pltpu.HBM)
SMEM = pl.BlockSpec(memory_space=pltpu.SMEM)


def block_product(a, b):
    a_hi, b_hi = a.astype(jnp.bfloat16), b.astype(jnp.bfloat16)
    a_lo = (a - a_hi.astype(jnp.float32)).astype(jnp.bfloat16)
    b_lo = (b - b_hi.astype(jnp.float32)).astype(jnp.bfloat16)

    def dot(left, right):
        return jnp.dot(left, right, preferred_element_type=jnp.float32)

    return dot(a_hi, b_hi) + (dot(a_hi, b_lo) + dot(a_lo, b_hi))


def plan_later(slots, kept, plan):
    touched = [jnp.int32(0)] * F
    for p in range(SLOTS):
        v = slots[0, 0, p]
        for q in range(SLOTS):
            w = slots[1, 0, q]
            target = jnp.where((v < 16) & (w < 16) & ((v & 3) == (w >> 2)), (v & 12) + (w & 3), -1)
            place = jnp.int32(F)
            for f in range(F):
                mine = kept[0, 0, f] == target
                place = jnp.where(mine, f, place)
                touched[f] = jnp.where(mine, 1, touched[f])
            plan[p * SLOTS + q] = place
    for f in range(F):
        plan[TOUCHED + f] = touched[f]


def wanted_slot(f, p, a_slots, b_slots, kept):
    v, block = a_slots[0, 0, p], kept[0, 0, f]
    wanted = jnp.where((v < 16) & ((v & 12) == (block & 12)), (v & 3) * 4 + (block & 3), -1)
    q = jnp.int32(SLOTS)
    for slot in range(SLOTS):
        q = jnp.where(b_slots[0, 0, slot] == wanted, slot, q)
    return q


def exchange_kernel(a_ref, b_ref, ai_ref, bi_ref, ci_ref, a2_ref, b2_ref, c0_ref, plan_ref, msg, got, slots, a_here, b_here,
                    c_here, beside, l_sems, c_sems, relay, first, second,
                    a_sems, i_sems, up_send, up_recv, on_send, on_recv, b_sems, f_sems, s_sems, h_sems, m_sems, t_sems, g_sems,
                    ready):
    row, col = lax.axis_index("row"), lax.axis_index("col")
    y, z_lo = lax.rem(row, LINES), lax.div(row, LINES)
    core, chip = lax.rem(col, 2), lax.div(col, 2)
    z_hi, x = lax.rem(chip, 4), lax.div(chip, 4)
    z = z_hi * 4 + z_lo
    core0, core1 = core == 0, core == 1

    def place(px, py, pz, pcore):
        pz = lax.rem(pz, ZS)
        return (lax.rem(pz, 4) * LINES + py, (lax.rem(px, 4) * 4 + lax.div(pz, 4)) * 2 + pcore)

    def when(*conditions):
        whole = conditions[0]
        for condition in conditions[1:]:
            whole = whole & condition
        return pl.when(whole)

    def one(*conditions):
        whole = conditions[0]
        for condition in conditions[1:]:
            whole = whole & condition
        return jnp.where(whole, 1, 0)

    a_to, a_from = (row, lax.rem(col + 31, 32)), (row, lax.rem(col + 1, 32))
    relay_to = place(x, y, z + UP, 0)
    sender_z = lax.rem(z + ZS - UP, ZS)
    sender_hi = lax.div(sender_z, 4)
    sender = place(x, y, z + ZS - UP, 0)
    relay_end = place(x + jnp.where(sender_hi == 0, 3, 0), y, sender_z + 12, 1)
    last_relay = place(x + jnp.where(z_hi == 3, 1, 0), y, z + 4 + UP, 0)
    from_z = lax.rem(z + 4, ZS)

    def share(at, table=SHARE):
        found = at * 0
        for place_z, count in enumerate(table):
            if count:
                found = found + jnp.where(at == place_z, count, 0)
        return found

    my_share, relay_share, from_share = share(z), share(sender_z), share(from_z)
    my_side, from_side = share(z, SIDE), share(from_z, SIDE)
    side_to, side_from = (row, lax.rem(col + 30, 32)), (row, lax.rem(col + 2, 32))

    sends_up, relays, gets_up = core0 & (my_share > 0), core0 & (relay_share > 0), core1 & (from_share > 0)
    up_late = z + UP < ZS
    in_late = z >= UP
    on_late = z < 4 + UP
    got_late = z >= 12 - UP
    down_late, end_late = z_hi == 0, z_hi == 3

    z_down, z_up = lax.rem(z_lo + 3, 4) * LINES, lax.rem(z_lo + 1, 4) * LINES
    here = z_lo * LINES
    top, bottom = y == 0, y == LINES - 1
    b_to = (lax.rem(row + 31, 32), col)
    b_from = (lax.rem(row + 1, 32), col)
    col0, col1 = col - core, col - core + 1

    barrier = pltpu.get_barrier_semaphore()

    def greet(device):
        pl.semaphore_signal(barrier, inc=1, device_id=device, device_id_type=MESH)

    @when(~bottom)
    def _():
        greet(b_from)

    @when(core0)
    def _():
        greet(a_from)

    @when(core1, ~end_late)
    def _():
        greet(a_from)

    @when(core1, from_side > 0)
    def _():
        greet(side_from)

    @when(core1, my_side > 0)
    def _():
        greet((row, col0))

    @when(core0, down_late)
    def _():
        greet(a_to)

    @when(sends_up, up_late)
    def _():
        greet(relay_to)

    @when(relays, ~in_late)
    def _():
        greet(sender)

    @when(relays, on_late)
    def _():
        greet(relay_end)

    @when(gets_up, ~got_late)
    def _():
        greet(last_relay)

    @when(top)
    def _():
        for line in range(1, LINES):
            greet((here + line, col1))
        greet((z_down, col1))
        greet(b_to)

    @when(core1, ~top, ~bottom)
    def _():
        greet((z_up + y, col1))

    @when(bottom)
    def _():
        for line in range(LINES - 1):
            greet((here + line, col1))
        greet((z_up + LINES - 1, col1))

    fetch_a = pltpu.make_async_copy(a_ref, a_here, l_sems.at[0])
    fetch_b = pltpu.make_async_copy(b_ref, b_here, l_sems.at[1])
    fetch_a.start()
    fetch_b.start()

    ints = (8, 128)
    lane = lax.broadcasted_iota(jnp.int32, ints, 1)
    for which, source in enumerate((ai_ref, bi_ref)):
        packed = jnp.zeros(ints, jnp.int32)
        for slot in range(SLOTS):
            packed = jnp.where(lane == slot, source[0, 0, slot], packed)
        msg[which] = packed

    greetings = one(~top) + one(core1) + one(core0, ~down_late) + one(core1, end_late)
    greetings = greetings + one(sends_up, ~up_late) + one(relays, in_late) + one(relays, ~on_late)
    greetings = greetings + one(gets_up, got_late) + 4 * one(core1) + one(core1, ~top, ~bottom)
    greetings = greetings + one(bottom) + one(my_side > 0)
    @when(greetings > 0)
    def _():
        pl.semaphore_wait(barrier, greetings)

    def tell(which, device):
        pl.semaphore_signal(ready.at[which], inc=1, device_id=device, device_id_type=MESH)

    @when(core1, end_late)
    def _():
        tell(0, a_from)

    @when(core1, ~top)
    def _():
        tell(3, (here, col0))
        tell(3, (here, col1))

    @when(core1, top)
    def _():
        tell(3, (z_up, col0))
        tell(3, (z_up, col1))

    @when(bottom)
    def _():
        tell(3, b_from)

    @when(relays, in_late)
    def _():
        tell(1, sender)

    @when(gets_up, got_late)
    def _():
        tell(2, last_relay)

    def remote(src, dst, send, recv, device):
        return pltpu.make_async_remote_copy(src_ref=src, dst_ref=dst, send_sem=send, recv_sem=recv,
                                            device_id=device, device_id_type=MESH)

    def head(g, side):
        rows = pl.ds(0, (ALL - g - side) * CHUNK)
        return remote(a_ref.at[rows], a2_ref.at[rows], a_sems.at[0], a_sems.at[1], a_to)

    def across(g, side):
        rows = pl.ds((ALL - g - side) * CHUNK, side * CHUNK)
        return remote(a_ref.at[rows], beside.at[pl.ds(0, side * CHUNK)], a_sems.at[2], a_sems.at[3], (row, col1))

    def aside(g, side):
        rows = pl.ds((ALL - g - side) * CHUNK, side * CHUNK)
        return remote(beside.at[pl.ds(0, side * CHUNK)], a2_ref.at[rows], a_sems.at[4], a_sems.at[5], side_to)

    def chunk_rows(g, n):
        return pl.ds(ROWS - g * CHUNK + n * CHUNK, CHUNK)

    def slot_rows(n):
        return pl.ds(n * CHUNK, CHUNK)

    def up(g, n):
        return remote(a_ref.at[chunk_rows(g, n)], relay.at[slot_rows(n)], up_send.at[n], up_recv.at[n], relay_to)

    def on(g, n):
        return remote(relay.at[slot_rows(n)], a2_ref.at[chunk_rows(g, n)], on_send.at[n], on_recv.at[n], relay_end)

    whole = remote(a_ref, a2_ref, a_sems.at[0], a_sems.at[1], a_to)
    ints_a = remote(msg.at[0], got.at[0], i_sems.at[0], i_sems.at[1], a_to)
    ints_b = remote(msg.at[1], got.at[1], i_sems.at[2], i_sems.at[3], b_to)
    b_main = remote(b_ref, b2_ref, b_sems.at[0], b_sems.at[1], b_to)

    def part(line):
        return pl.ds(line * PIECE, PIECE)

    my_part = pl.ds(pl.multiple_of(y * PIECE, PIECE), PIECE)

    def leg_y(line, c):
        return remote(b_ref.at[part(line)], first.at[c], f_sems.at[line], h_sems.at[c], (here + line, col1))

    def leg_z(c):
        return remote(b_ref.at[part(0)], second.at[c], f_sems.at[0], s_sems.at[c], (z_down, col1))

    def then_z(c):
        return remote(first.at[c], second.at[c], m_sems.at[c], s_sems.at[c], (z_down + y, col1))

    def then_end(c):
        return remote(first.at[c], b2_ref.at[part(LINES - 1)], m_sems.at[c], g_sems.at[LINES - 1],
                      (z_down + LINES - 1, col0 + c))

    def then_y(c):
        return remote(second.at[c], b2_ref.at[my_part], t_sems.at[c], g_sems.at[y], (here + LINES - 1, col0 + c))

    def arrival(line):
        return remote(second.at[0], b2_ref.at[part(line)], t_sems.at[0], g_sems.at[line], (here, col))

    @when(core1)
    def _():
        whole.start()

    @when(~top)
    def _():
        b_main.start()
        ints_b.start()

    @when(core1)
    def _():
        ints_a.start()

    for g, side in PAIRS:
        @when(core0, my_share == g, my_side == side)
        def _():
            if side:
                across(g, side).start()

            @when(~down_late)
            def _():
                ints_a.start()
                if g + side < ALL:
                    head(g, side).start()

    for g, side in PAIRS:
        if side:
            @when(core1, my_share == g, my_side == side)
            def _():
                across(g, side).wait_recv()
                aside(g, side).start()

    def kept_block(f, carry):
        total = jnp.zeros((BS, BS), jnp.float32)
        for p in range(SLOTS):
            q = wanted_slot(f, p, ai_ref, bi_ref, ci_ref)
            right = jnp.zeros((BS, BS), jnp.float32)
            for slot in range(SLOTS):
                right = jnp.where(q == slot, b_here[pl.ds(slot * BS, BS), :], right)
            total = total + block_product(a_here[pl.ds(p * BS, BS), :], right)
        c_here[f] = total
        return carry

    stores = [pltpu.make_async_copy(c_here.at[f], c0_ref.at[f], c_sems.at[f]) for f in range(F)]

    def early(first_f, last_f):
        lax.fori_loop(first_f, last_f, kept_block, 0)
        for f in range(first_f, last_f):
            stores[f].start()

    fetch_a.wait()
    fetch_b.wait()
    early(0, HALF)

    for c in range(2):
        @when(top, core == c)
        def _():
            pl.semaphore_wait(ready.at[3], LINES + 1)
            for line in (4, 3, 5, 2, 6, 1, 7):
                leg_y(line, c).start()
            leg_z(c).start()
            ints_b.start()

    @when(sends_up, up_late)
    def _():
        pl.semaphore_wait(ready.at[1], 1)

    for g in COUNTS:
        if g:
            @when(core0, my_share == g)
            def _():
                for n in range(g):
                    up(g, n).start()

    @when(core0, down_late)
    def _():
        pl.semaphore_wait(ready.at[0], 1)
        ints_a.start()

    for g, side in PAIRS:
        if g + side < ALL:
            @when(core0, down_late, my_share == g, my_side == side)
            def _():
                head(g, side).start()

    @when(core0)
    def _():
        early(HALF, F)

    @when(relays, on_late)
    def _():
        pl.semaphore_wait(ready.at[2], 1)

    for g in COUNTS:
        if g:
            @when(core0, relay_share == g)
            def _():
                for n in range(g):
                    up(g, n).wait_recv()
                    on(g, n).start()

    for c in range(2):
        @when(core1, ~top)
        def _():
            leg_y(1, c).wait_recv()

        @when(core1, ~top, ~bottom)
        def _():
            then_z(c).start()

        @when(core1, bottom)
        def _():
            then_end(c).start()

    @when(core1)
    def _():
        early(HALF, F)

    for c in range(2):
        @when(core1, ~bottom)
        def _():
            leg_z(c).wait_recv()
            then_y(c).start()

    ints_a.wait()
    ints_b.wait()
    fetch_slots = pltpu.make_async_copy(got, slots, l_sems.at[2])
    fetch_slots.start()
    fetch_slots.wait()
    plan_later(slots, ci_ref, plan_ref)

    @when(core1)
    def _():
        whole.wait_send()

    @when(core0)
    def _():
        whole.wait_recv()

    @when(~top)
    def _():
        b_main.wait_send()

    @when(~bottom)
    def _():
        b_main.wait_recv()

    @when(top)
    def _():
        leg_z(0).wait_send()
        for line in range(1, LINES):
            leg_y(line, 0).wait_send()

    for c in range(2):
        @when(core1, ~top)
        def _():
            then_z(c).wait_send()

        @when(core1, ~bottom)
        def _():
            then_y(c).wait_send()

    @when(bottom)
    def _():
        for line in range(LINES):
            arrival(line).wait_recv()

    for g, side in PAIRS:
        @when(core0, my_share == g, my_side == side)
        def _():
            for n in range(g):
                up(g, n).wait_send()
            if g + side < ALL:
                head(g, side).wait_send()
            if side:
                across(g, side).wait_send()

        @when(core1, from_share == g, from_side == side)
        def _():
            if g + side < ALL:
                head(g, side).wait_recv()
            if side:
                aside(g, side).wait_recv()

        if side:
            @when(core1, my_share == g, my_side == side)
            def _():
                aside(g, side).wait_send()

    for g in COUNTS:
        if g:
            @when(core0, relay_share == g)
            def _():
                for n in range(g):
                    on(g, n).wait_send()

            @when(core1, from_share == g)
            def _():
                for n in range(g):
                    on(g, n).wait_recv()

    for f in range(F):
        stores[f].wait()


def exchange(a, b, a_index, b_index, c_index):
    panel = jax.ShapeDtypeStruct((ROWS, BS), jnp.float32)
    blocks = jax.ShapeDtypeStruct((F, BS, BS), jnp.float32)
    plan = jax.ShapeDtypeStruct((PLAN,), jnp.int32)
    dma = pltpu.SemaphoreType.DMA
    return pl.pallas_call(
        exchange_kernel,
        out_shape=(panel, panel, blocks, plan),
        in_specs=[HBM, HBM, SMEM, SMEM, SMEM],
        out_specs=(HBM, HBM, HBM, SMEM),
        scratch_shapes=[
            pltpu.VMEM((2, 8, 128), jnp.int32),
            pltpu.VMEM((2, 8, 128), jnp.int32),
            pltpu.SMEM((2, 8, 128), jnp.int32),
            pltpu.VMEM((ROWS, BS), jnp.float32),
            pltpu.VMEM((ROWS, BS), jnp.float32),
            pltpu.VMEM((F, BS, BS), jnp.float32),
            pltpu.VMEM((max(1, max(SIDE)) * CHUNK, BS), jnp.float32),
            dma((3,)),
            dma((F,)),
            pltpu.VMEM((MOST * CHUNK, BS), jnp.float32),
            pltpu.VMEM((2, PIECE, BS), jnp.float32),
            pltpu.VMEM((2, PIECE, BS), jnp.float32),
            dma((6,)),
            dma((4,)),
            dma((MOST,)),
            dma((MOST,)),
            dma((MOST,)),
            dma((MOST,)),
            dma((2,)),
            dma((LINES,)),
            dma((2,)),
            dma((2,)),
            dma((2,)),
            dma((2,)),
            dma((LINES,)),
            pltpu.SemaphoreType.REGULAR((4,)),
        ],
        compiler_params=pltpu.CompilerParams(collective_id=0, has_side_effects=True, vmem_limit_bytes=VMEM),
        cost_estimate=pl.CostEstimate(flops=6 * F * SLOTS * BS ** 3, bytes_accessed=12 * ROWS * BS * 4, transcendentals=0),
        name="exchange",
    )(a, b, a_index, b_index, c_index)


def product_kernel(c0, a1, b1, plan_ref, out, plan, va, vb, acc, todo, p_sem, a_sem, b_sem, in_sem, out_sem):
    fetch_plan = pltpu.make_async_copy(plan_ref, plan, p_sem)
    fetch_plan.start()
    starts = [pltpu.make_async_copy(c0.at[f], acc.at[f], in_sem.at[f]) for f in range(F)]
    writes = [pltpu.make_async_copy(acc.at[f], out.at[f], out_sem.at[f]) for f in range(F)]
    fetches = [pltpu.make_async_copy(a1, va, a_sem), pltpu.make_async_copy(b1, vb, b_sem)]
    for copy in starts + fetches:
        copy.start()
    fetch_plan.wait()
    touched = [plan[TOUCHED + f] for f in range(F)]
    count = jnp.int32(0)
    for p in range(SLOTS):
        for q in range(SLOTS):
            place = plan[p * SLOTS + q]
            todo[count] = (p * 4 + q) * 8 + place
            count = count + jnp.where(place < F, 1, 0)

    for f in range(F):
        starts[f].wait()
        pl.when(touched[f] == 0)(writes[f].start)
    for copy in fetches:
        copy.wait()

    def pair(t, carry):
        entry = todo[t]
        f = entry & 7
        left = va[pl.ds(pl.multiple_of((entry >> 5) * BS, BS), BS), :]
        right = vb[pl.ds(pl.multiple_of(((entry >> 3) & 3) * BS, BS), BS), :]
        acc[f] += block_product(left, right)
        return carry

    lax.fori_loop(0, count, pair, 0)
    for f in range(F):
        pl.when(touched[f] != 0)(writes[f].start)
    for f in range(F):
        writes[f].wait()


def products(c0, a1, b1, plan):
    dma = pltpu.SemaphoreType.DMA
    return pl.pallas_call(
        product_kernel,
        out_shape=jax.ShapeDtypeStruct((F, BS, BS), jnp.float32),
        in_specs=[HBM, HBM, HBM, HBM],
        out_specs=HBM,
        scratch_shapes=[
            pltpu.SMEM((PLAN,), jnp.int32),
            pltpu.VMEM((ROWS, BS), jnp.float32),
            pltpu.VMEM((ROWS, BS), jnp.float32),
            pltpu.VMEM((F, BS, BS), jnp.float32),
            pltpu.SMEM((SLOTS * SLOTS + 1,), jnp.int32),
            dma,
            dma,
            dma,
            dma((F,)),
            dma((F,)),
        ],
        compiler_params=pltpu.CompilerParams(vmem_limit_bytes=VMEM),
        cost_estimate=pl.CostEstimate(flops=6 * BS ** 3, bytes_accessed=12 * BS * BS * 4, transcendentals=0),
        name="products",
    )(c0, a1, b1, plan)


def per_device(a_panels, a_index, b_panels, b_index, c_index):
    a0 = a_panels.reshape(ROWS, BS)
    b0 = b_panels.reshape(ROWS, BS)
    a1, b1, c0, plan = exchange(a0, b0, a_index, b_index, c_index)
    blocks = products(c0, a1, b1, plan)
    return blocks[None, None]


def solution(mesh):
    return jax.shard_map(
        per_device,
        mesh=mesh,
        in_specs=(
            P("row", "col", None, None, None),
            P("row", "col", None),
            P("row", "col", None, None, None),
            P("row", "col", None),
            P("row", "col", None),
        ),
        out_specs=P("row", "col", None, None, None),
        check_vma=False,
    )
```
